128 devices in a mesh: nodes: 128 (over x, z, y, core).
Axes of the slice: x: 4, y: 4, z: 4, core: 2. Of those that a mesh axis runs over, the one named last changes fastest.
Arguments:
- features: bfloat16 [131072, 512], P('nodes'), may hold values from -6 to 6
- preact: float32 [131072, 512], P('nodes'), may hold values from -6 to 6
- cotangent: float32 [131072, 512], P('nodes'), may hold values from -6 to 6
- w_self: float32 [512, 512], replicated, may hold values from -0.25 to 0.25
- w_neigh: float32 [512, 512], replicated, may hold values from -0.25 to 0.25
- tile_counts: int32 [1024, 10, 128, 128], P('nodes'), may hold values from 0 to 2, as said below
- tile_col: int32 [1024, 10], P('nodes'), may hold values from 0 to 71, as said below
- boundary_owner: int32 [128, 64], P('nodes'), may hold values from 0 to 127, as said below
- boundary_slot: int32 [128, 64], P('nodes'), may hold values from 0 to 7
Outputs:
- grad_features: float32 [131072, 512], P('nodes')
- grad_self: float32 [512, 512], replicated
- grad_neigh: float32 [512, 512], replicated
The draws below stay inside these ranges and needn't reach their ends.
Inputs may be any that keep to these rules, and one draw needn't show every extreme that they name: `tile_col`: values below 8 name one of the device's own blocks, value 8 + k its boundary block k; every boundary block of a device is named by at least one tile of that device's row blocks. `boundary_owner`: the 64 boundary blocks of one device have distinct owners, none of them the device itself. `tile_counts`: most entries are zero.
All inputs are finite; a program needn't handle non-finite values.
Results may differ from the reference program's by a relative error of at most 0.007.
Values may be sent and summed in bfloat16 or wider, within the bound.
No kernel may reach another device: no remote copies, remote signals or barrier semaphores. Data moves between devices by JAX's collectives and lax.ppermute only.
A program may use at most 256 MiB of HBM per device.

```python
import math
import jax
import jax.numpy as jnp
from jax import lax

D = 512
BLK = 128
BLK_DEV = 8
OWNERS = 128
NB = 64
K = 10
COLUMNS = 72
NBLOCKS = 1024
NODES = 131072


def draw_tile_counts(key, part):
    key = jax.random.fold_in(key, 7)
    entry_key, value_key, row_key = jax.random.split(key, 3)
    shape = (NBLOCKS, K, BLK, BLK)
    present = jax.random.randint(entry_key, shape, 0, BLK, dtype=jnp.int32) < 3
    values = jax.random.randint(value_key, shape, 1, 3, dtype=jnp.int32)
    live_rows = jax.random.randint(row_key, (NBLOCKS, K, BLK, 1), 0, 16, dtype=jnp.int32) > 0
    return jnp.where(present & live_rows, values, 0).astype(jnp.int32)


def draw_tile_col(key, part):
    key = jax.random.fold_in(key, 11)
    positions = BLK_DEV * K

    def one_device(dev_key):
        order_key, pick_key = jax.random.split(dev_key)
        chosen = jax.random.randint(pick_key, (positions,), 0, BLK_DEV + NB, dtype=jnp.int32)
        places = jnp.arange(positions, dtype=jnp.int32)
        initial = jnp.where(places < NB, BLK_DEV + places, chosen)
        shuffle = jax.random.permutation(order_key, positions)
        return initial[shuffle].reshape(BLK_DEV, K)
    device_keys = jax.random.split(key, NBLOCKS // BLK_DEV)
    return jax.vmap(one_device)(device_keys).reshape(NBLOCKS, K).astype(jnp.int32)


def draw_boundary_owner(key, part):
    key = jax.random.fold_in(key, 23)

    def one_device(dev_key, device):
        others = jax.random.permutation(dev_key, OWNERS - 1)[:NB].astype(jnp.int32)
        return others + (others >= device).astype(jnp.int32)
    device_keys = jax.random.split(key, OWNERS)
    return jax.vmap(one_device)(device_keys, jnp.arange(OWNERS, dtype=jnp.int32))


def plant(result, stream_key, smallest, high):
    extent = result.shape
    spot = [jax.random.randint(jax.random.fold_in(stream_key, axis), (), 0, extent[axis]) for axis in range(len(extent))]
    result = result.at[tuple(spot)].set(smallest)
    longest = extent.index(max(extent))
    spot[longest] = (spot[longest] + 1) % extent[longest]
    return result.at[tuple(spot)].set(high)


def block_levels(key, dims, cuts, least, top_value):
    loudness = 1.0
    for dim, blocks in cuts:
        draws = jax.random.uniform(jax.random.fold_in(jax.random.fold_in(key, 6), dim), (blocks,), jnp.float32, least / len(cuts), top_value / len(cuts))
        loudness = loudness * jnp.repeat(jnp.exp(draws), dims[dim] // blocks).reshape((-1,) + (1,) * (len(dims) - 1 - dim))
    return loudness


def noise(rng, extent, scale, bound, shards=(), kind=jnp.bfloat16):
    drawn = jax.random.normal(rng, extent, jnp.float32) * scale
    if len(shards) > 0:
        drawn = block_levels(rng, extent, shards, -0.22, 0.18) * drawn
    return jnp.clip(drawn, min=-bound, max=bound).astype(kind)


def setup_inputs(seed: int = 0) -> dict:
    key_list = jax.random.split(jax.random.key(seed), 10)
    return {
        "features": noise(key_list[0], (NODES, D), 1.0, 6.0, ((0, 128),)),
        "preact": noise(key_list[1], (NODES, D), 1.0, 6.0, ((0, 128),), jnp.float32),
        "cotangent": noise(key_list[2], (NODES, D), 1.0, 6.0, ((0, 128),), jnp.float32),
        "w_self": noise(key_list[3], (D, D), D ** -0.5, 0.25, (), jnp.float32),
        "w_neigh": noise(key_list[4], (D, D), D ** -0.5, 0.25, (), jnp.float32),
        "tile_counts": draw_tile_counts(jax.random.fold_in(key_list[9], 71), 0),
        "tile_col": draw_tile_col(jax.random.fold_in(key_list[9], 71), 0),
        "boundary_owner": draw_boundary_owner(jax.random.fold_in(key_list[9], 71), 0),
        "boundary_slot": plant(jax.random.randint(key_list[8], (OWNERS, NB), 0, BLK_DEV), jax.random.fold_in(key_list[8], 1), 0, BLK_DEV - 1).astype(jnp.int32),
    }


PRECISE = lax.Precision.HIGHEST

def normalized_tiles(counts):
    values = counts.astype(jnp.float32)
    degree = 1.0 + lax.optimization_barrier(jnp.sum(values, axis=(1, 3)))
    return values / jnp.sqrt(degree)[:, None, :, None]

def reference(features, preact, cotangent, w_self, w_neigh, tile_counts, tile_col, boundary_owner, boundary_slot):
    grad_pre = jnp.where(preact > 0, cotangent, jnp.zeros_like(cotangent))
    blocks = features.astype(jnp.float32).reshape(NBLOCKS, BLK, D)
    back_neigh = jnp.dot(grad_pre, w_neigh.T, precision=PRECISE).reshape(NBLOCKS, BLK, D)
    grad_blocks = grad_pre.reshape(NBLOCKS, BLK, D)
    column_ids = jnp.arange(COLUMNS, dtype=jnp.int32)

    def per_device(totals, device):
        returned, neigh_sum = totals
        first_block = (device * BLK_DEV).astype(jnp.int32)
        remote_ids = (boundary_owner[device] * BLK_DEV + boundary_slot[device]).astype(jnp.int32)
        local_ids = first_block + jnp.arange(BLK_DEV, dtype=jnp.int32)
        lookup = jnp.concatenate([local_ids, remote_ids])
        tile_cols = lax.dynamic_slice_in_dim(tile_col, first_block, BLK_DEV, 0)
        weights = normalized_tiles(lax.dynamic_slice_in_dim(tile_counts, first_block, BLK_DEV, 0))
        gathered = blocks[lookup[tile_cols]]
        aggregated = jnp.einsum('bkij,bkjd->bid', weights, gathered, precision=PRECISE)
        own_grad = lax.dynamic_slice_in_dim(grad_blocks, first_block, BLK_DEV, 0)
        neigh_sum = neigh_sum + jnp.dot(aggregated.reshape(-1, D).T, own_grad.reshape(-1, D), precision=PRECISE)
        own_back = lax.dynamic_slice_in_dim(back_neigh, first_block, BLK_DEV, 0)
        contrib = jnp.einsum('bkij,bid->bkjd', weights, own_back, precision=PRECISE)
        one_hot = (tile_cols[:, :, None] == column_ids[None, None, :]).astype(jnp.float32)
        binned = jnp.einsum('bkc,bkjd->cjd', one_hot, contrib, precision=PRECISE)
        rounded = lax.optimization_barrier(binned[BLK_DEV:].astype(jnp.bfloat16))
        remote_part = rounded.astype(jnp.float32)
        current = lax.dynamic_slice_in_dim(returned, first_block, BLK_DEV, 0)
        returned = lax.dynamic_update_slice_in_dim(returned, current + binned[:BLK_DEV], first_block, 0)
        returned = returned.at[remote_ids].add(remote_part)
        return ((returned, neigh_sum), None)
    start_state = (jnp.zeros((NBLOCKS, BLK, D), jnp.float32), jnp.zeros((D, D), jnp.float32))
    (returned, neigh_total), unused = lax.scan(per_device, start_state, jnp.arange(NBLOCKS // BLK_DEV, dtype=jnp.int32))
    norm_factor = 1.0 / math.sqrt(NODES)
    grad_self = jnp.dot(features.astype(jnp.float32).T, grad_pre, precision=PRECISE) * norm_factor
    grad_neigh = neigh_total * norm_factor
    grad_features = jnp.dot(grad_pre, w_self.T, precision=PRECISE) + returned.reshape(NODES, D)
    return (grad_features, grad_self, grad_neigh)
```

```python
import functools
import math

import jax
import jax.numpy as jnp
from jax import lax
from jax.experimental import pallas as pl
from jax.experimental.pallas import tpu as pltpu
from jax.sharding import PartitionSpec as P

D = 512
BLK = 128
BLK_DEV = 8
OWNERS = 128
NB = 64
K = 10
COLUMNS = BLK_DEV + NB
F32 = jnp.float32
BF16 = jnp.bfloat16


def dot(a, b):
    return lax.dot_general(a, b, (((1,), (0,)), ((), ())), preferred_element_type=F32)


def halves(values):
    upper = values.astype(BF16)
    return upper, (values - upper.astype(F32)).astype(BF16)


def scatter_kernel(col_ref, owner_ref, counts_ref, preact_ref, cot_ref, own_ref, send_ref, acc, stage, sems):
    b = pl.program_id(0)

    @pl.when(b == 0)
    def _():
        acc[...] = jnp.zeros_like(acc)

    counts = counts_ref[0].astype(F32)
    degree = 1.0 + jnp.sum(jnp.sum(counts, axis=0), axis=1, keepdims=True)
    grad = jnp.where(preact_ref[...] > 0, cot_ref[...], 0.0) / jnp.sqrt(degree)
    upper, lower = halves(grad.T)
    both = jnp.concatenate([upper, lower], axis=1)
    tiles = counts.astype(BF16)
    for t in range(0, K, 2):
        pair = jnp.concatenate([tiles[t], tiles[t + 1]], axis=1)
        part = dot(both, jnp.concatenate([pair, pair], axis=0))
        acc[col_ref[b, t]] += part[:, :BLK]
        acc[col_ref[b, t + 1]] += part[:, BLK:]

    @pl.when(b == BLK_DEV - 1)
    def _():
        own_ref[...] = acc[:BLK_DEV]

        def put(k):
            return pltpu.make_async_copy(stage.at[k], send_ref.at[owner_ref[k]], sems.at[k])

        @pl.loop(0, NB)
        def _(k):
            stage[k] = acc[BLK_DEV + k].astype(BF16)
            put(k).start()

        @pl.loop(0, NB)
        def _(k):
            put(k).wait()


def partials(tile_col, owners, counts, preact, cotangent):
    return pl.pallas_call(
        scatter_kernel,
        grid_spec=pltpu.PrefetchScalarGridSpec(
            num_scalar_prefetch=2,
            grid=(BLK_DEV,),
            in_specs=[
                pl.BlockSpec((1, K, BLK, BLK), lambda b, *_: (b, 0, 0, 0)),
                pl.BlockSpec((BLK, D), lambda b, *_: (b, 0)),
                pl.BlockSpec((BLK, D), lambda b, *_: (b, 0)),
            ],
            out_specs=[
                pl.BlockSpec((BLK_DEV, D, BLK), lambda b, *_: (0, 0, 0)),
                pl.BlockSpec(memory_space=pl.ANY),
            ],
            scratch_shapes=[
                pltpu.VMEM((COLUMNS, D, BLK), F32),
                pltpu.VMEM((NB, D, BLK), BF16),
                pltpu.SemaphoreType.DMA((NB,)),
            ],
        ),
        out_shape=[
            jax.ShapeDtypeStruct((BLK_DEV, D, BLK), F32),
            jax.ShapeDtypeStruct((OWNERS, D, BLK), BF16),
        ],
        compiler_params=pltpu.CompilerParams(vmem_limit_bytes=56 << 20),
        cost_estimate=pl.CostEstimate(
            flops=4 * BLK_DEV * K * BLK * BLK * D, bytes_accessed=20 << 20, transcendentals=0
        ),
    )(tile_col, owners, counts, preact, cotangent)


GROUP = 8


def gather_kernel(asked_ref, recv_ref, own_ref, base_ref, feat_ref, weight_ref, grad_ref, neigh_ref, acc):
    step = pl.program_id(0)

    @pl.when(step == 0)
    def _():
        acc[...] = own_ref[...]

    for i in range(GROUP):
        slot = asked_ref[step * GROUP + i]

        @pl.when(slot >= 0)
        def _():
            acc[slot] += recv_ref[i].astype(F32)

    @pl.when(step == OWNERS // GROUP - 1)
    def _():
        w_upper, w_lower = halves(weight_ref[...])
        neigh_ref[...] = jnp.zeros_like(neigh_ref)
        for g in range(0, BLK_DEV, 2):
            total = jnp.concatenate([acc[g], acc[g + 1]], axis=1)
            upper, lower = halves(total)
            rows = slice(g * BLK, (g + 2) * BLK)
            feat = feat_ref[rows, :]
            neigh_ref[...] += dot(upper, feat) + dot(lower, feat)
            upper, lower = halves(total.T)
            grad_ref[rows, :] = base_ref[rows, :] + (
                dot(upper, w_upper) + dot(lower, w_upper) + dot(upper, w_lower)
            )


def totals(asked, received, own, base, features, weight):
    whole = lambda *shape: pl.BlockSpec(shape, lambda s, *_: (0,) * len(shape))
    return pl.pallas_call(
        gather_kernel,
        grid_spec=pltpu.PrefetchScalarGridSpec(
            num_scalar_prefetch=1,
            grid=(OWNERS // GROUP,),
            in_specs=[
                pl.BlockSpec((GROUP, D, BLK), lambda s, *_: (s, 0, 0)),
                whole(BLK_DEV, D, BLK),
                whole(BLK_DEV * BLK, D),
                whole(BLK_DEV * BLK, D),
                whole(D, D),
            ],
            out_specs=[whole(BLK_DEV * BLK, D), whole(D, D)],
            scratch_shapes=[pltpu.VMEM((BLK_DEV, D, BLK), F32)],
        ),
        out_shape=[
            jax.ShapeDtypeStruct((BLK_DEV * BLK, D), F32),
            jax.ShapeDtypeStruct((D, D), F32),
        ],
        compiler_params=pltpu.CompilerParams(vmem_limit_bytes=48 << 20),
        cost_estimate=pl.CostEstimate(
            flops=10 * BLK_DEV * BLK * D * D, bytes_accessed=26 << 20, transcendentals=0
        ),
    )(asked, received, own, base, features, weight)


def sum_everywhere(values):
    rows = D // OWNERS
    shares = lax.all_to_all(values.reshape(OWNERS, rows, D), "nodes", 0, 0, tiled=True)
    share = jnp.sum(shares, axis=0)
    spread = jnp.broadcast_to(share[None], (OWNERS, rows, D))
    return lax.all_to_all(spread, "nodes", 0, 0, tiled=True).reshape(D, D)


def shards(features, preact, cotangent, w_self, w_neigh, tile_counts, tile_col, owner, slot):
    me = lax.axis_index("nodes")
    lists = lax.all_gather(owner * BLK_DEV + slot, "nodes", axis=0, tiled=True)
    own, outgoing = partials(tile_col, owner[0], tile_counts, preact, cotangent)
    received = lax.all_to_all(outgoing, "nodes", 0, 0, tiled=True)

    asked = jnp.max(jnp.where(lists // BLK_DEV == me, lists % BLK_DEV, -1), axis=1)
    grad_pre = jnp.where(preact > 0, cotangent, 0.0)
    upper, lower = halves(grad_pre)
    w_upper, w_lower = halves(w_self.T)
    base = dot(upper, w_upper) + dot(lower, w_upper) + dot(upper, w_lower)
    turned = features.T
    self_part = dot(turned, upper) + dot(turned, lower)
    self_total = lax.psum(self_part, "nodes")

    grad_features, neigh_part = totals(asked, received, own, base, features, w_neigh.T)
    neigh_total = sum_everywhere(neigh_part).T
    scale = 1.0 / math.sqrt(OWNERS * BLK_DEV * BLK)
    return grad_features, self_total * scale, neigh_total * scale


def solution(mesh):
    rows = P("nodes", None)
    return jax.shard_map(
        shards,
        mesh=mesh,
        in_specs=(rows, rows, rows, P(), P(), P("nodes", None, None, None), rows, rows, rows),
        out_specs=(rows, P(), P()),
        check_vma=False,
    )
```

```python
import functools
import math

import jax
import jax.numpy as jnp
from jax import lax
from jax.experimental import pallas as pl
from jax.experimental.pallas import tpu as pltpu
from jax.sharding import PartitionSpec as P

D = 512
BLK = 128
BLK_DEV = 8
OWNERS = 128
NB = 64
K = 10
COLUMNS = BLK_DEV + NB
TAG = 16
F32 = jnp.float32
BF16 = jnp.bfloat16


def dot(a, b):
    return lax.dot_general(a, b, (((1,), (0,)), ((), ())), preferred_element_type=F32)


def halves(values):
    upper = values.astype(BF16)
    return upper, (values - upper.astype(F32)).astype(BF16)


def scatter_kernel(
    col_ref, owner_ref, slot_ref, counts_ref, preact_ref, cot_ref, own_ref, send_ref, acc, stage, tags, sems, tag_sem
):
    b = pl.program_id(0)
    untagged = pltpu.make_async_copy(tags, send_ref.at[:, pl.ds(D, TAG), :], tag_sem)

    @pl.when(b == 0)
    def _():
        acc[...] = jnp.zeros_like(acc)
        tags[...] = jnp.full_like(tags, -1)
        untagged.start()

    counts = counts_ref[0].astype(F32)
    degree = 1.0 + jnp.sum(jnp.sum(counts, axis=0), axis=1, keepdims=True)
    grad = jnp.where(preact_ref[...] > 0, cot_ref[...], 0.0) / jnp.sqrt(degree)
    upper, lower = halves(grad.T)
    both = jnp.concatenate([upper, lower], axis=1)
    tiles = counts.astype(BF16)
    for t in range(0, K, 2):
        pair = jnp.concatenate([tiles[t], tiles[t + 1]], axis=1)
        part = dot(both, jnp.concatenate([pair, pair], axis=0))
        acc[col_ref[b, t]] += part[:, :BLK]
        acc[col_ref[b, t + 1]] += part[:, BLK:]

    @pl.when(b == BLK_DEV - 1)
    def _():
        own_ref[...] = acc[:BLK_DEV]
        untagged.wait()

        def put(k):
            return pltpu.make_async_copy(stage.at[k], send_ref.at[owner_ref[k]], sems.at[k])

        @pl.loop(0, NB)
        def _(k):
            stage[k, :D] = acc[BLK_DEV + k].astype(BF16)
            stage[k, D:] = jnp.full((TAG, BLK), slot_ref[k].astype(F32), F32).astype(BF16)
            put(k).start()

        @pl.loop(0, NB)
        def _(k):
            put(k).wait()


def partials(tile_col, owners, slots, counts, preact, cotangent):
    return pl.pallas_call(
        scatter_kernel,
        grid_spec=pltpu.PrefetchScalarGridSpec(
            num_scalar_prefetch=3,
            grid=(BLK_DEV,),
            in_specs=[
                pl.BlockSpec((1, K, BLK, BLK), lambda b, *_: (b, 0, 0, 0)),
                pl.BlockSpec((BLK, D), lambda b, *_: (b, 0)),
                pl.BlockSpec((BLK, D), lambda b, *_: (b, 0)),
            ],
            out_specs=[
                pl.BlockSpec((BLK_DEV, D, BLK), lambda b, *_: (0, 0, 0)),
                pl.BlockSpec(memory_space=pl.ANY),
            ],
            scratch_shapes=[
                pltpu.VMEM((COLUMNS, D, BLK), F32),
                pltpu.VMEM((NB, D + TAG, BLK), BF16),
                pltpu.VMEM((OWNERS, TAG, BLK), BF16),
                pltpu.SemaphoreType.DMA((NB,)),
                pltpu.SemaphoreType.DMA,
            ],
        ),
        out_shape=[
            jax.ShapeDtypeStruct((BLK_DEV, D, BLK), F32),
            jax.ShapeDtypeStruct((OWNERS, D + TAG, BLK), BF16),
        ],
        compiler_params=pltpu.CompilerParams(vmem_limit_bytes=56 << 20),
        cost_estimate=pl.CostEstimate(
            flops=4 * BLK_DEV * K * BLK * BLK * D, bytes_accessed=20 << 20, transcendentals=0
        ),
    )(tile_col, owners, slots, counts, preact, cotangent)


GROUP = 8


def gather_kernel(asked_ref, recv_ref, own_ref, feat_ref, total_ref, neigh_ref):
    step = pl.program_id(0)

    @pl.when(step == 0)
    def _():
        total_ref[...] = own_ref[...]

    for i in range(GROUP):
        slot = asked_ref[step * GROUP + i]

        @pl.when(slot >= 0)
        def _():
            total_ref[slot] += recv_ref[i, :D].astype(F32)

    @pl.when(step == OWNERS // GROUP - 1)
    def _():
        neigh_ref[...] = jnp.zeros_like(neigh_ref)
        for g in range(0, BLK_DEV, 2):
            upper, lower = halves(jnp.concatenate([total_ref[g], total_ref[g + 1]], axis=1))
            feat = feat_ref[g * BLK : (g + 2) * BLK, :]
            neigh_ref[...] += dot(upper, feat) + dot(lower, feat)


def whole(*shape):
    return pl.BlockSpec(shape, lambda *_: (0,) * len(shape))


def totals(asked, received, own, features):
    return pl.pallas_call(
        gather_kernel,
        grid_spec=pltpu.PrefetchScalarGridSpec(
            num_scalar_prefetch=1,
            grid=(OWNERS // GROUP,),
            in_specs=[
                pl.BlockSpec((GROUP, D + TAG, BLK), lambda s, *_: (s, 0, 0)),
                whole(BLK_DEV, D, BLK),
                whole(BLK_DEV * BLK, D),
            ],
            out_specs=[whole(BLK_DEV, D, BLK), whole(D, D)],
        ),
        out_shape=[
            jax.ShapeDtypeStruct((BLK_DEV, D, BLK), F32),
            jax.ShapeDtypeStruct((D, D), F32),
        ],
        compiler_params=pltpu.CompilerParams(vmem_limit_bytes=40 << 20),
        cost_estimate=pl.CostEstimate(
            flops=4 * BLK_DEV * BLK * D * D, bytes_accessed=20 << 20, transcendentals=0
        ),
    )(asked, received, own, features)


def feature_kernel(total_ref, base_ref, weight_ref, grad_ref):
    w_upper, w_lower = halves(weight_ref[...].T)
    upper, lower = halves(jnp.concatenate([total_ref[0], total_ref[1]], axis=1).T)
    grad_ref[...] = base_ref[...] + (dot(upper, w_upper) + dot(lower, w_upper) + dot(upper, w_lower))


def feature_gradient(total, base, weight):
    return pl.pallas_call(
        feature_kernel,
        grid=(BLK_DEV // 2,),
        in_specs=[
            pl.BlockSpec((2, D, BLK), lambda g: (g, 0, 0)),
            pl.BlockSpec((2 * BLK, D), lambda g: (g, 0)),
            whole(D, D),
        ],
        out_specs=pl.BlockSpec((2 * BLK, D), lambda g: (g, 0)),
        out_shape=jax.ShapeDtypeStruct((BLK_DEV * BLK, D), F32),
        compiler_params=pltpu.CompilerParams(vmem_limit_bytes=32 << 20),
        cost_estimate=pl.CostEstimate(
            flops=6 * BLK_DEV * BLK * D * D, bytes_accessed=7 << 20, transcendentals=0
        ),
    )(total, base, weight)


def sum_everywhere(values):
    rows = values.shape[0] // OWNERS
    shares = lax.all_to_all(values.astype(BF16).reshape(OWNERS, rows, D), "nodes", 0, 0, tiled=True)
    share = jnp.sum(shares.astype(F32), axis=0).astype(BF16)
    spread = jnp.broadcast_to(share[None], (OWNERS, rows, D))
    return lax.all_to_all(spread, "nodes", 0, 0, tiled=True).reshape(-1, D).astype(F32)


def shards(features, preact, cotangent, w_self, w_neigh, tile_counts, tile_col, owner, slot):
    own, outgoing = partials(tile_col, owner[0], slot[0], tile_counts, preact, cotangent)
    received = lax.all_to_all(outgoing, "nodes", 0, 0, tiled=True)

    grad_pre = jnp.where(preact > 0, cotangent, 0.0)
    upper, lower = halves(grad_pre)
    turned = features.T
    self_part = dot(turned, upper) + dot(turned, lower)
    w_upper, w_lower = halves(w_self.T)
    base = dot(upper, w_upper) + dot(lower, w_upper) + dot(upper, w_lower)

    asked = received[:, D, 0].astype(jnp.int32)
    total, neigh_part = totals(asked, received, own, features)
    both = sum_everywhere(jnp.concatenate([self_part, neigh_part], axis=0))
    grad_features = feature_gradient(total, base, w_neigh)
    scale = 1.0 / math.sqrt(OWNERS * BLK_DEV * BLK)
    return grad_features, both[:D] * scale, both[D:].T * scale


def solution(mesh):
    rows = P("nodes", None)
    return jax.shard_map(
        shards,
        mesh=mesh,
        in_specs=(rows, rows, rows, P(), P(), P("nodes", None, None, None), rows, rows, rows),
        out_specs=(rows, P(), P()),
        check_vma=False,
    )
```

```python
import functools
import math

import jax
import jax.numpy as jnp
from jax import lax
from jax.experimental import pallas as pl
from jax.experimental.pallas import tpu as pltpu
from jax.sharding import PartitionSpec as P

D = 512
BLK = 128
BLK_DEV = 8
OWNERS = 128
NB = 64
K = 10
COLUMNS = BLK_DEV + NB
TAG = 16
F32 = jnp.float32
BF16 = jnp.bfloat16


def dot(a, b):
    return lax.dot_general(a, b, (((1,), (0,)), ((), ())), preferred_element_type=F32)


def halves(values):
    upper = values.astype(BF16)
    return upper, (values - upper.astype(F32)).astype(BF16)


def scatter_kernel(
    col_ref, owner_ref, slot_ref, counts_ref, preact_ref, cot_ref, own_ref, send_ref, acc, stage, tags, sems, tag_sem
):
    b = pl.program_id(0)
    untagged = pltpu.make_async_copy(tags, send_ref.at[:, pl.ds(D, TAG), :], tag_sem)

    @pl.when(b == 0)
    def _():
        acc[...] = jnp.zeros_like(acc)
        tags[...] = jnp.full_like(tags, -1)
        untagged.start()

    counts = counts_ref[0].astype(F32)
    degree = 1.0 + jnp.sum(jnp.sum(counts, axis=0), axis=1, keepdims=True)
    grad = jnp.where(preact_ref[...] > 0, cot_ref[...], 0.0) / jnp.sqrt(degree)
    upper, lower = halves(grad.T)
    both = jnp.concatenate([upper, lower], axis=1)
    tiles = counts.astype(BF16)
    for t in range(0, K, 2):
        pair = jnp.concatenate([tiles[t], tiles[t + 1]], axis=1)
        part = dot(both, jnp.concatenate([pair, pair], axis=0))
        acc[col_ref[b, t]] += part[:, :BLK]
        acc[col_ref[b, t + 1]] += part[:, BLK:]

    @pl.when(b == BLK_DEV - 1)
    def _():
        own_ref[...] = acc[:BLK_DEV]
        untagged.wait()

        def put(k):
            return pltpu.make_async_copy(stage.at[k], send_ref.at[owner_ref[k]], sems.at[k])

        @pl.loop(0, NB)
        def _(k):
            stage[k, :D] = acc[BLK_DEV + k].astype(BF16)
            stage[k, D:] = jnp.full((TAG, BLK), slot_ref[k].astype(F32), F32).astype(BF16)
            put(k).start()

        @pl.loop(0, NB)
        def _(k):
            put(k).wait()


def partials(tile_col, owners, slots, counts, preact, cotangent):
    return pl.pallas_call(
        scatter_kernel,
        grid_spec=pltpu.PrefetchScalarGridSpec(
            num_scalar_prefetch=3,
            grid=(BLK_DEV,),
            in_specs=[
                pl.BlockSpec((1, K, BLK, BLK), lambda b, *_: (b, 0, 0, 0)),
                pl.BlockSpec((BLK, D), lambda b, *_: (b, 0)),
                pl.BlockSpec((BLK, D), lambda b, *_: (b, 0)),
            ],
            out_specs=[
                pl.BlockSpec((BLK_DEV, D, BLK), lambda b, *_: (0, 0, 0)),
                pl.BlockSpec(memory_space=pl.ANY),
            ],
            scratch_shapes=[
                pltpu.VMEM((COLUMNS, D, BLK), F32),
                pltpu.VMEM((NB, D + TAG, BLK), BF16),
                pltpu.VMEM((OWNERS, TAG, BLK), BF16),
                pltpu.SemaphoreType.DMA((NB,)),
                pltpu.SemaphoreType.DMA,
            ],
        ),
        out_shape=[
            jax.ShapeDtypeStruct((BLK_DEV, D, BLK), F32),
            jax.ShapeDtypeStruct((OWNERS, D + TAG, BLK), BF16),
        ],
        compiler_params=pltpu.CompilerParams(vmem_limit_bytes=56 << 20),
        cost_estimate=pl.CostEstimate(
            flops=4 * BLK_DEV * K * BLK * BLK * D, bytes_accessed=20 << 20, transcendentals=0
        ),
    )(tile_col, owners, slots, counts, preact, cotangent)


GROUP = 8


def gather_kernel(asked_ref, recv_ref, own_ref, feat_ref, total_ref, neigh_ref):
    step = pl.program_id(0)

    @pl.when(step == 0)
    def _():
        total_ref[...] = own_ref[...]

    for i in range(GROUP):
        slot = asked_ref[step * GROUP + i]

        @pl.when(slot >= 0)
        def _():
            total_ref[slot] += recv_ref[i, :D].astype(F32)

    @pl.when(step == OWNERS // GROUP - 1)
    def _():
        neigh_ref[...] = jnp.zeros_like(neigh_ref)
        for g in range(0, BLK_DEV, 2):
            upper, lower = halves(jnp.concatenate([total_ref[g], total_ref[g + 1]], axis=1))
            feat = feat_ref[g * BLK : (g + 2) * BLK, :]
            neigh_ref[...] += dot(upper, feat) + dot(lower, feat)


def whole(*shape):
    return pl.BlockSpec(shape, lambda *_: (0,) * len(shape))


def totals(asked, received, own, features):
    return pl.pallas_call(
        gather_kernel,
        grid_spec=pltpu.PrefetchScalarGridSpec(
            num_scalar_prefetch=1,
            grid=(OWNERS // GROUP,),
            in_specs=[
                pl.BlockSpec((GROUP, D + TAG, BLK), lambda s, *_: (s, 0, 0)),
                whole(BLK_DEV, D, BLK),
                whole(BLK_DEV * BLK, D),
            ],
            out_specs=[whole(BLK_DEV, D, BLK), whole(D, D)],
        ),
        out_shape=[
            jax.ShapeDtypeStruct((BLK_DEV, D, BLK), F32),
            jax.ShapeDtypeStruct((D, D), F32),
        ],
        compiler_params=pltpu.CompilerParams(vmem_limit_bytes=40 << 20),
        cost_estimate=pl.CostEstimate(
            flops=4 * BLK_DEV * BLK * D * D, bytes_accessed=20 << 20, transcendentals=0
        ),
    )(asked, received, own, features)


def feature_kernel(total_ref, base_ref, weight_ref, grad_ref):
    w_upper, w_lower = halves(weight_ref[...].T)
    upper, lower = halves(jnp.concatenate([total_ref[0], total_ref[1]], axis=1).T)
    grad_ref[...] = base_ref[...] + (dot(upper, w_upper) + dot(lower, w_upper) + dot(upper, w_lower))


def feature_gradient(total, base, weight):
    return pl.pallas_call(
        feature_kernel,
        grid=(BLK_DEV // 2,),
        in_specs=[
            pl.BlockSpec((2, D, BLK), lambda g: (g, 0, 0)),
            pl.BlockSpec((2 * BLK, D), lambda g: (g, 0)),
            whole(D, D),
        ],
        out_specs=pl.BlockSpec((2 * BLK, D), lambda g: (g, 0)),
        out_shape=jax.ShapeDtypeStruct((BLK_DEV * BLK, D), F32),
        compiler_params=pltpu.CompilerParams(vmem_limit_bytes=32 << 20),
        cost_estimate=pl.CostEstimate(
            flops=6 * BLK_DEV * BLK * D * D, bytes_accessed=7 << 20, transcendentals=0
        ),
    )(total, base, weight)


def sum_everywhere(values):
    rows = values.shape[0] // OWNERS
    shares = lax.all_to_all(values.astype(BF16).reshape(OWNERS, rows, D), "nodes", 0, 0, tiled=True)
    share = jnp.sum(shares.astype(F32), axis=0).astype(BF16)
    spread = jnp.broadcast_to(share[None], (OWNERS, rows, D))
    return lax.all_to_all(spread, "nodes", 0, 0, tiled=True).reshape(-1, D).astype(F32)


def shards(features, preact, cotangent, w_self, w_neigh, tile_counts, tile_col, owner, slot):
    own, outgoing = partials(tile_col, owner[0], slot[0], tile_counts, preact, cotangent)
    grad_pre = jnp.where(preact > 0, cotangent, 0.0)
    upper, lower = halves(grad_pre)
    turned = features.T
    self_part = dot(turned, upper) + dot(turned, lower)
    w_upper, w_lower = halves(w_self.T)
    base = dot(upper, w_upper) + dot(lower, w_upper) + dot(upper, w_lower)

    outgoing, self_part, base = lax.optimization_barrier((outgoing, self_part, base))
    received = lax.all_to_all(outgoing, "nodes", 0, 0, tiled=True)
    received, self_part, base = lax.optimization_barrier((received, self_part, base))

    asked = received[:, D, 0].astype(jnp.int32)
    total, neigh_part = totals(asked, received, own, features)
    both = sum_everywhere(jnp.concatenate([self_part, neigh_part], axis=0))
    grad_features = feature_gradient(total, base, w_neigh)
    scale = 1.0 / math.sqrt(OWNERS * BLK_DEV * BLK)
    return grad_features, both[:D] * scale, both[D:].T * scale


def solution(mesh):
    rows = P("nodes", None)
    return jax.shard_map(
        shards,
        mesh=mesh,
        in_specs=(rows, rows, rows, P(), P(), P("nodes", None, None, None), rows, rows, rows),
        out_specs=(rows, P(), P()),
        check_vma=False,
    )
```

```python
import functools
import math

import jax
import jax.numpy as jnp
from jax import lax
from jax.experimental import pallas as pl
from jax.experimental.pallas import tpu as pltpu
from jax.sharding import PartitionSpec as P

D = 512
BLK = 128
BLK_DEV = 8
OWNERS = 128
NB = 64
K = 10
COLUMNS = BLK_DEV + NB
TAG = 16
F32 = jnp.float32
BF16 = jnp.bfloat16


def dot(a, b):
    return lax.dot_general(a, b, (((1,), (0,)), ((), ())), preferred_element_type=F32)


def halves(values):
    upper = values.astype(BF16)
    return upper, (values - upper.astype(F32)).astype(BF16)


def whole(*shape):
    return pl.BlockSpec(shape, lambda *_: (0,) * len(shape))


def scatter_kernel(
    col_ref,
    owner_ref,
    slot_ref,
    counts_ref,
    preact_ref,
    cot_ref,
    feat_ref,
    own_ref,
    self_ref,
    send_ref,
    acc,
    stage,
    tags,
    sems,
    tag_sem,
):
    b = pl.program_id(0)
    untagged = pltpu.make_async_copy(tags, send_ref.at[:, pl.ds(D, TAG), :], tag_sem)

    @pl.when(b == 0)
    def _():
        acc[...] = jnp.zeros_like(acc)
        self_ref[...] = jnp.zeros_like(self_ref)
        tags[...] = jnp.full_like(tags, -1)
        untagged.start()

    counts = counts_ref[0].astype(F32)
    degree = 1.0 + jnp.sum(jnp.sum(counts, axis=0), axis=1, keepdims=True)
    root = jnp.broadcast_to(jnp.sqrt(degree), (BLK, BLK)).T[:1]
    grad = jnp.where(preact_ref[...] > 0, cot_ref[...], 0.0).T
    both = jnp.concatenate(halves(grad), axis=1)
    feat = feat_ref[...]
    self_ref[...] += dot(both, jnp.concatenate([feat, feat], axis=0))
    both = jnp.concatenate(halves(grad / root), axis=1)
    tiles = counts.astype(BF16)
    for t in range(0, K, 2):
        pair = jnp.concatenate([tiles[t], tiles[t + 1]], axis=1)
        part = dot(both, jnp.concatenate([pair, pair], axis=0))
        acc[col_ref[b, t]] += part[:, :BLK]
        acc[col_ref[b, t + 1]] += part[:, BLK:]

    @pl.when(b == BLK_DEV - 1)
    def _():
        untagged.wait()

        def put(k):
            return pltpu.make_async_copy(stage.at[k], send_ref.at[owner_ref[k]], sems.at[k])

        @pl.loop(0, NB)
        def _(k):
            stage[k, :D] = acc[BLK_DEV + k].astype(BF16)
            stage[k, D:] = jnp.full((TAG, BLK), slot_ref[k].astype(F32), F32).astype(BF16)
            put(k).start()

        own_ref[...] = acc[:BLK_DEV]
        self_ref[...] = self_ref[...].T

        @pl.loop(0, NB)
        def _(k):
            put(k).wait()


def partials(tile_col, owners, slots, counts, preact, cotangent, features):
    rows = pl.BlockSpec((BLK, D), lambda b, *_: (b, 0))
    return pl.pallas_call(
        scatter_kernel,
        grid_spec=pltpu.PrefetchScalarGridSpec(
            num_scalar_prefetch=3,
            grid=(BLK_DEV,),
            in_specs=[pl.BlockSpec((1, K, BLK, BLK), lambda b, *_: (b, 0, 0, 0)), rows, rows, rows],
            out_specs=[whole(BLK_DEV, D, BLK), whole(D, D), pl.BlockSpec(memory_space=pl.ANY)],
            scratch_shapes=[
                pltpu.VMEM((COLUMNS, D, BLK), F32),
                pltpu.VMEM((NB, D + TAG, BLK), BF16),
                pltpu.VMEM((OWNERS, TAG, BLK), BF16),
                pltpu.SemaphoreType.DMA((NB,)),
                pltpu.SemaphoreType.DMA,
            ],
        ),
        out_shape=[
            jax.ShapeDtypeStruct((BLK_DEV, D, BLK), F32),
            jax.ShapeDtypeStruct((D, D), F32),
            jax.ShapeDtypeStruct((OWNERS, D + TAG, BLK), BF16),
        ],
        compiler_params=pltpu.CompilerParams(vmem_limit_bytes=58 << 20),
        cost_estimate=pl.CostEstimate(
            flops=4 * BLK_DEV * K * BLK * BLK * D, bytes_accessed=22 << 20, transcendentals=0
        ),
    )(tile_col, owners, slots, counts, preact, cotangent, features)


GROUP = 8
STEPS = OWNERS // GROUP
SHARE = BLK_DEV * D // STEPS


def gather_kernel(asked_ref, recv_ref, own_ref, feat_ref, self_ref, total_ref, joined_ref):
    step = pl.program_id(0)

    @pl.when(step == 0)
    def _():
        total_ref[...] = jnp.zeros_like(total_ref)

    for i in range(GROUP):
        slot = asked_ref[step * GROUP + i]

        @pl.when(slot >= 0)
        def _():
            total_ref[slot] += recv_ref[i, :D].astype(F32)

    share = pl.ds(pl.multiple_of(step % (D // SHARE) * SHARE, SHARE), SHARE)
    total_ref[step // (D // SHARE), share] += own_ref[0]

    @pl.when(step == STEPS - 1)
    def _():
        neigh = jnp.zeros((D, D), F32)
        for g in range(0, BLK_DEV, 2):
            upper, lower = halves(jnp.concatenate([total_ref[g], total_ref[g + 1]], axis=1))
            feat = feat_ref[g * BLK : (g + 2) * BLK, :]
            neigh += dot(upper, feat) + dot(lower, feat)
        joined_ref[:D] = self_ref[...].astype(BF16)
        joined_ref[D:] = neigh.T.astype(BF16)


def totals(asked, received, own, features, self_part):
    return pl.pallas_call(
        gather_kernel,
        grid_spec=pltpu.PrefetchScalarGridSpec(
            num_scalar_prefetch=1,
            grid=(STEPS,),
            in_specs=[
                pl.BlockSpec((GROUP, D + TAG, BLK), lambda s, *_: (s, 0, 0)),
                pl.BlockSpec((1, SHARE, BLK), lambda s, *_: (s, 0, 0)),
                whole(BLK_DEV * BLK, D),
                whole(D, D),
            ],
            out_specs=[whole(BLK_DEV, D, BLK), whole(2 * D, D)],
        ),
        out_shape=[
            jax.ShapeDtypeStruct((BLK_DEV, D, BLK), F32),
            jax.ShapeDtypeStruct((2 * D, D), BF16),
        ],
        compiler_params=pltpu.CompilerParams(vmem_limit_bytes=20 << 20),
        cost_estimate=pl.CostEstimate(
            flops=4 * BLK_DEV * BLK * D * D, bytes_accessed=20 << 20, transcendentals=0
        ),
    )(asked, received, own.reshape(STEPS, SHARE, BLK), features, self_part)


def feature_kernel(total_ref, preact_ref, cot_ref, self_ref, neigh_ref, grad_ref):
    grad = jnp.where(preact_ref[...] > 0, cot_ref[...], 0.0)
    upper, lower = halves(grad)
    w_upper, w_lower = halves(self_ref[...].T)
    result = dot(upper, w_upper) + dot(lower, w_upper) + dot(upper, w_lower)
    upper, lower = halves(jnp.concatenate([total_ref[0], total_ref[1]], axis=1).T)
    w_upper, w_lower = halves(neigh_ref[...].T)
    grad_ref[...] = result + (dot(upper, w_upper) + dot(lower, w_upper) + dot(upper, w_lower))


def feature_gradient(total, preact, cotangent, w_self, w_neigh):
    rows = pl.BlockSpec((2 * BLK, D), lambda g: (g, 0))
    return pl.pallas_call(
        feature_kernel,
        grid=(BLK_DEV // 2,),
        in_specs=[pl.BlockSpec((2, D, BLK), lambda g: (g, 0, 0)), rows, rows, whole(D, D), whole(D, D)],
        out_specs=rows,
        out_shape=jax.ShapeDtypeStruct((BLK_DEV * BLK, D), F32),
        compiler_params=pltpu.CompilerParams(vmem_limit_bytes=16 << 20),
        cost_estimate=pl.CostEstimate(
            flops=12 * BLK_DEV * BLK * D * D, bytes_accessed=10 << 20, transcendentals=0
        ),
    )(total, preact, cotangent, w_self, w_neigh)


def shards(features, preact, cotangent, w_self, w_neigh, tile_counts, tile_col, owner, slot):
    own, self_part, outgoing = partials(tile_col, owner[0], slot[0], tile_counts, preact, cotangent, features)
    received = lax.all_to_all(outgoing, "nodes", 0, 0, tiled=True)
    asked = received[:, D, 0].astype(jnp.int32)
    total, joined = totals(asked, received, own, features, self_part)

    rows = 2 * D // OWNERS
    shares = lax.all_to_all(joined.reshape(OWNERS, rows, D), "nodes", 0, 0, tiled=True)
    share = jnp.sum(shares.astype(F32), axis=0).astype(BF16)
    share, total = lax.optimization_barrier((share, total))
    spread = jnp.broadcast_to(share[None], (OWNERS, rows, D))
    both = lax.all_to_all(spread, "nodes", 0, 0, tiled=True).reshape(2 * D, D)
    grad_features = feature_gradient(total, preact, cotangent, w_self, w_neigh)
    scale = 1.0 / math.sqrt(OWNERS * BLK_DEV * BLK)
    return grad_features, both[:D].astype(F32) * scale, both[D:].astype(F32) * scale


def solution(mesh):
    rows = P("nodes", None)
    return jax.shard_map(
        shards,
        mesh=mesh,
        in_specs=(rows, rows, rows, P(), P(), P("nodes", None, None, None), rows, rows, rows),
        out_specs=(rows, P(), P()),
        check_vma=False,
    )
```

```python
import functools
import math

import jax
import jax.numpy as jnp
from jax import lax
from jax.experimental import pallas as pl
from jax.experimental.pallas import tpu as pltpu
from jax.sharding import PartitionSpec as P

D = 512
BLK = 128
BLK_DEV = 8
OWNERS = 128
NB = 64
K = 10
COLUMNS = BLK_DEV + NB
TAG = 16
PIECES = D // OWNERS
SENT = PIECES * NB + TAG
BATCH = 16
F32 = jnp.float32
BF16 = jnp.bfloat16


def dot(a, b):
    return lax.dot_general(a, b, (((1,), (0,)), ((), ())), preferred_element_type=F32)


def halves(values):
    upper = values.astype(BF16)
    return upper, (values - upper.astype(F32)).astype(BF16)


def whole(*shape):
    return pl.BlockSpec(shape, lambda *_: (0,) * len(shape))


def scatter_kernel(
    col_ref, counts_ref, preact_ref, cot_ref, feat_ref, tag_ref, own_ref, self_ref, send_ref, acc, stage, sems
):
    b = pl.program_id(0)

    @pl.when(b == 0)
    def _():
        acc[...] = jnp.zeros_like(acc)
        self_ref[...] = jnp.zeros_like(self_ref)

    counts = counts_ref[0].astype(F32)
    degree = 1.0 + jnp.sum(jnp.sum(counts, axis=0), axis=1, keepdims=True)
    root = jnp.broadcast_to(jnp.sqrt(degree), (BLK, BLK)).T[:1]
    grad = jnp.where(preact_ref[...] > 0, cot_ref[...], 0.0).T
    both = jnp.concatenate(halves(grad), axis=1)
    feat = feat_ref[...]
    self_ref[...] += dot(both, jnp.concatenate([feat, feat], axis=0))
    both = jnp.concatenate(halves(grad / root), axis=1)
    tiles = counts.astype(BF16)

    def column(c):
        return pl.ds(pl.multiple_of(c * D, D), D)

    for t in range(0, K, 2):
        pair = jnp.concatenate([tiles[t], tiles[t + 1]], axis=1)
        part = dot(both, jnp.concatenate([pair, pair], axis=0))
        acc[column(col_ref[b, t])] += part[:, :BLK]
        acc[column(col_ref[b, t + 1])] += part[:, BLK:]

    @pl.when(b == BLK_DEV - 1)
    def _():
        def put(g):
            rows = pl.ds(g * BATCH, BATCH)
            return pltpu.make_async_copy(stage.at[rows], send_ref.at[rows], sems.at[g])

        @pl.loop(0, OWNERS // BATCH)
        def _(g):
            @pl.loop(0, BATCH)
            def _(i):
                j = g * BATCH + i
                for r in range(PIECES):
                    start = BLK_DEV * D + r * OWNERS + j
                    stage[j, r * NB : (r + 1) * NB] = acc[pl.ds(start, NB, stride=D)].astype(BF16)
                stage[j, PIECES * NB :] = tag_ref[...]

            put(g).start()

        own_ref[...] = acc[: BLK_DEV * D].reshape(BLK_DEV, D, BLK)
        self_ref[...] = self_ref[...].T

        @pl.loop(0, OWNERS // BATCH)
        def _(g):
            put(g).wait()


def partials(tile_col, counts, preact, cotangent, features, tag):
    rows = pl.BlockSpec((BLK, D), lambda b, *_: (b, 0))
    return pl.pallas_call(
        scatter_kernel,
        grid_spec=pltpu.PrefetchScalarGridSpec(
            num_scalar_prefetch=1,
            grid=(BLK_DEV,),
            in_specs=[
                pl.BlockSpec((1, K, BLK, BLK), lambda b, *_: (b, 0, 0, 0)),
                rows,
                rows,
                rows,
                whole(TAG, BLK),
            ],
            out_specs=[whole(BLK_DEV, D, BLK), whole(D, D), pl.BlockSpec(memory_space=pl.ANY)],
            scratch_shapes=[
                pltpu.VMEM((COLUMNS * D, BLK), F32),
                pltpu.VMEM((OWNERS, SENT, BLK), BF16),
                pltpu.SemaphoreType.DMA((OWNERS // BATCH,)),
            ],
        ),
        out_shape=[
            jax.ShapeDtypeStruct((BLK_DEV, D, BLK), F32),
            jax.ShapeDtypeStruct((D, D), F32),
            jax.ShapeDtypeStruct((OWNERS, SENT, BLK), BF16),
        ],
        compiler_params=pltpu.CompilerParams(vmem_limit_bytes=58 << 20),
        cost_estimate=pl.CostEstimate(
            flops=4 * BLK_DEV * K * BLK * BLK * D, bytes_accessed=22 << 20, transcendentals=0
        ),
    )(tile_col, counts, preact, cotangent, features, tag)


GROUP = 16
STEPS = OWNERS // GROUP
BINS = OWNERS * BLK_DEV
MERGED = 256


def merge_kernel(ids_ref, recv_ref, out_ref, acc):
    step = pl.program_id(0)

    @pl.when(step == 0)
    def _():
        acc[...] = jnp.zeros_like(acc)

    pieces = [recv_ref[:, r * NB : (r + 1) * NB].reshape(GROUP * NB, BLK) for r in range(PIECES)]
    values = jnp.concatenate(pieces, axis=1)
    rows = lax.broadcasted_iota(jnp.int32, (MERGED, BLK), 0)
    for m in range(0, BINS, MERGED):
        hot = [
            jnp.where(rows == ids_ref[p : p + 1] - m, 1.0, 0.0).astype(BF16) for p in range(GROUP // 2)
        ]
        acc[m : m + MERGED] += dot(jnp.concatenate(hot, axis=1), values)

    @pl.when(step == STEPS - 1)
    def _():
        out_ref[...] = acc[...].astype(BF16)


def merged(ids, received):
    return pl.pallas_call(
        merge_kernel,
        grid=(STEPS,),
        in_specs=[
            pl.BlockSpec((GROUP // 2, BLK), lambda s: (s, 0)),
            pl.BlockSpec((GROUP, SENT, BLK), lambda s: (s, 0, 0)),
        ],
        out_specs=whole(BINS, PIECES * BLK),
        out_shape=jax.ShapeDtypeStruct((BINS, PIECES * BLK), BF16),
        scratch_shapes=[pltpu.VMEM((BINS, PIECES * BLK), F32)],
        compiler_params=pltpu.CompilerParams(vmem_limit_bytes=24 << 20),
        cost_estimate=pl.CostEstimate(
            flops=2 * BINS * OWNERS * NB * PIECES * BLK, bytes_accessed=10 << 20, transcendentals=0
        ),
    )(ids, received)


def total_kernel(recv_ref, own_ref, feat_ref, self_ref, total_ref, joined_ref, flat):
    arrived = recv_ref[...].astype(F32).reshape(BINS, PIECES * BLK)
    for r in range(PIECES):
        flat[r * BINS : (r + 1) * BINS] = arrived[:, r * BLK : (r + 1) * BLK]
    for g in range(BLK_DEV):
        for r in range(PIECES):
            rows = slice(r * OWNERS, (r + 1) * OWNERS)
            part = flat[pl.ds(r * BINS + g, OWNERS, stride=BLK_DEV)]
            total_ref[g, rows] = own_ref[g, rows] + part
    neigh = jnp.zeros((D, D), F32)
    for g in range(0, BLK_DEV, 2):
        upper, lower = halves(jnp.concatenate([total_ref[g], total_ref[g + 1]], axis=1))
        feat = feat_ref[g * BLK : (g + 2) * BLK, :]
        neigh += dot(upper, feat) + dot(lower, feat)
    joined_ref[:D] = self_ref[...].astype(BF16)
    joined_ref[D:] = neigh.T.astype(BF16)


def totals(received, own, features, self_part):
    return pl.pallas_call(
        total_kernel,
        in_specs=[pl.BlockSpec(memory_space=pltpu.VMEM)] * 4,
        out_specs=[pl.BlockSpec(memory_space=pltpu.VMEM)] * 2,
        out_shape=[
            jax.ShapeDtypeStruct((BLK_DEV, D, BLK), F32),
            jax.ShapeDtypeStruct((2 * D, D), BF16),
        ],
        scratch_shapes=[pltpu.VMEM((PIECES * BINS, BLK), F32)],
        compiler_params=pltpu.CompilerParams(vmem_limit_bytes=24 << 20),
        cost_estimate=pl.CostEstimate(
            flops=4 * BLK_DEV * BLK * D * D, bytes_accessed=8 << 20, transcendentals=0
        ),
    )(received, own, features, self_part)


def feature_kernel(total_ref, preact_ref, cot_ref, self_ref, neigh_ref, grad_ref):
    grad = jnp.where(preact_ref[...] > 0, cot_ref[...], 0.0)
    upper, lower = halves(grad)
    w_upper, w_lower = halves(self_ref[...].T)
    result = dot(upper, w_upper) + dot(lower, w_upper) + dot(upper, w_lower)
    upper, lower = halves(jnp.concatenate([total_ref[0], total_ref[1]], axis=1).T)
    w_upper, w_lower = halves(neigh_ref[...].T)
    grad_ref[...] = result + (dot(upper, w_upper) + dot(lower, w_upper) + dot(upper, w_lower))


def feature_gradient(total, preact, cotangent, w_self, w_neigh):
    rows = pl.BlockSpec((2 * BLK, D), lambda g: (g, 0))
    return pl.pallas_call(
        feature_kernel,
        grid=(BLK_DEV // 2,),
        in_specs=[pl.BlockSpec((2, D, BLK), lambda g: (g, 0, 0)), rows, rows, whole(D, D), whole(D, D)],
        out_specs=rows,
        out_shape=jax.ShapeDtypeStruct((BLK_DEV * BLK, D), F32),
        compiler_params=pltpu.CompilerParams(vmem_limit_bytes=16 << 20),
        cost_estimate=pl.CostEstimate(
            flops=12 * BLK_DEV * BLK * D * D, bytes_accessed=10 << 20, transcendentals=0
        ),
    )(total, preact, cotangent, w_self, w_neigh)


def list_rows(owner, slot):
    lists = jnp.concatenate([owner, slot], axis=0)
    return jnp.pad(jnp.tile(lists, (1, BLK // NB)), ((0, TAG - 2), (0, 0))).astype(BF16)


def block_numbers(received):
    lists = received[:, PIECES * NB : PIECES * NB + 2].astype(jnp.int32)
    numbers = (lists[:, 0] * BLK_DEV + lists[:, 1]).reshape(OWNERS // 2, 2, BLK)
    lanes = lax.broadcasted_iota(jnp.int32, (OWNERS // 2, BLK), 1)
    return jnp.where(lanes < NB, numbers[:, 0], numbers[:, 1])


def shards(features, preact, cotangent, w_self, w_neigh, tile_counts, tile_col, owner, slot):
    own, self_part, outgoing = partials(
        tile_col, tile_counts, preact, cotangent, features, list_rows(owner, slot)
    )
    received = lax.all_to_all(outgoing, "nodes", 0, 0, tiled=True)
    sums = merged(block_numbers(received), received).reshape(OWNERS, BLK_DEV, PIECES * BLK)
    sums = lax.all_to_all(sums, "nodes", 0, 0, tiled=True)
    total, joined = totals(sums, own, features, self_part)

    rows = 2 * D // OWNERS
    shares = lax.all_to_all(joined.reshape(OWNERS, rows, D), "nodes", 0, 0, tiled=True)
    share = jnp.sum(shares.astype(F32), axis=0).astype(BF16)
    share, total = lax.optimization_barrier((share, total))
    spread = jnp.broadcast_to(share[None], (OWNERS, rows, D))
    both = lax.all_to_all(spread, "nodes", 0, 0, tiled=True).reshape(2 * D, D)
    grad_features = feature_gradient(total, preact, cotangent, w_self, w_neigh)
    scale = 1.0 / math.sqrt(OWNERS * BLK_DEV * BLK)
    return grad_features, both[:D].astype(F32) * scale, both[D:].astype(F32) * scale


def solution(mesh):
    rows = P("nodes", None)
    return jax.shard_map(
        shards,
        mesh=mesh,
        in_specs=(rows, rows, rows, P(), P(), P("nodes", None, None, None), rows, rows, rows),
        out_specs=(rows, P(), P()),
        check_vma=False,
    )
```

```python
import functools
import math

import jax
import jax.numpy as jnp
from jax import lax
from jax.experimental import pallas as pl
from jax.experimental.pallas import tpu as pltpu
from jax.sharding import PartitionSpec as P

D = 512
BLK = 128
BLK_DEV = 8
OWNERS = 128
NB = 64
K = 10
COLUMNS = BLK_DEV + NB
TAG = 16
PIECES = D // OWNERS
SENT = PIECES * NB + TAG
BATCH = 16
PITCH = D + 8
F32 = jnp.float32
BF16 = jnp.bfloat16


def dot(a, b):
    return lax.dot_general(a, b, (((1,), (0,)), ((), ())), preferred_element_type=F32)


def halves(values):
    upper = values.astype(BF16)
    return upper, (values - upper.astype(F32)).astype(BF16)


def whole(*shape):
    return pl.BlockSpec(shape, lambda *_: (0,) * len(shape))


def scatter_kernel(
    col_ref, counts_ref, preact_ref, cot_ref, feat_ref, tag_ref, own_ref, self_ref, send_ref, acc, stage, sems
):
    b = pl.program_id(0)

    @pl.when(b == 0)
    def _():
        acc[...] = jnp.zeros_like(acc)
        self_ref[...] = jnp.zeros_like(self_ref)

    counts = counts_ref[0].astype(F32)
    degree = 1.0 + jnp.sum(jnp.sum(counts, axis=0), axis=1, keepdims=True)
    root = jnp.broadcast_to(jnp.sqrt(degree), (BLK, BLK)).T[:1]
    grad = jnp.where(preact_ref[...] > 0, cot_ref[...], 0.0).T
    both = jnp.concatenate(halves(grad), axis=1)
    feat = feat_ref[...]
    self_ref[...] += dot(both, jnp.concatenate([feat, feat], axis=0))
    both = jnp.concatenate(halves(grad / root), axis=1)
    tiles = counts.astype(BF16)

    def column(c):
        return pl.ds(pl.multiple_of(c * PITCH, 8), D)

    for t in range(0, K, 2):
        pair = jnp.concatenate([tiles[t], tiles[t + 1]], axis=1)
        part = dot(both, jnp.concatenate([pair, pair], axis=0))
        acc[column(col_ref[b, t])] += part[:, :BLK]
        acc[column(col_ref[b, t + 1])] += part[:, BLK:]

    @pl.when(b == BLK_DEV - 1)
    def _():
        def put(g):
            rows = pl.ds(g * BATCH, BATCH)
            return pltpu.make_async_copy(stage.at[rows], send_ref.at[rows], sems.at[g])

        @pl.loop(0, OWNERS // BATCH)
        def _(g):
            @pl.loop(0, BATCH)
            def _(i):
                j = g * BATCH + i
                for r in range(PIECES):
                    start = BLK_DEV * PITCH + r * OWNERS + j
                    stage[j, r * NB : (r + 1) * NB] = acc[pl.ds(start, NB, stride=PITCH)].astype(BF16)
                stage[j, PIECES * NB :] = tag_ref[...]

            put(g).start()

        for c in range(BLK_DEV):
            own_ref[c] = acc[c * PITCH : c * PITCH + D]
        self_ref[...] = self_ref[...].T

        @pl.loop(0, OWNERS // BATCH)
        def _(g):
            put(g).wait()


def partials(tile_col, counts, preact, cotangent, features, tag):
    rows = pl.BlockSpec((BLK, D), lambda b, *_: (b, 0))
    return pl.pallas_call(
        scatter_kernel,
        grid_spec=pltpu.PrefetchScalarGridSpec(
            num_scalar_prefetch=1,
            grid=(BLK_DEV,),
            in_specs=[
                pl.BlockSpec((1, K, BLK, BLK), lambda b, *_: (b, 0, 0, 0)),
                rows,
                rows,
                rows,
                whole(TAG, BLK),
            ],
            out_specs=[whole(BLK_DEV, D, BLK), whole(D, D), pl.BlockSpec(memory_space=pl.ANY)],
            scratch_shapes=[
                pltpu.VMEM((COLUMNS * PITCH, BLK), F32),
                pltpu.VMEM((OWNERS, SENT, BLK), BF16),
                pltpu.SemaphoreType.DMA((OWNERS // BATCH,)),
            ],
        ),
        out_shape=[
            jax.ShapeDtypeStruct((BLK_DEV, D, BLK), F32),
            jax.ShapeDtypeStruct((D, D), F32),
            jax.ShapeDtypeStruct((OWNERS, SENT, BLK), BF16),
        ],
        compiler_params=pltpu.CompilerParams(vmem_limit_bytes=58 << 20),
        cost_estimate=pl.CostEstimate(
            flops=4 * BLK_DEV * K * BLK * BLK * D, bytes_accessed=22 << 20, transcendentals=0
        ),
    )(tile_col, counts, preact, cotangent, features, tag)


GROUP = 16
STEPS = OWNERS // GROUP
BINS = OWNERS * BLK_DEV
MERGED = 256


def merge_kernel(recv_ref, out_ref, acc):
    step = pl.program_id(0)

    @pl.when(step == 0)
    def _():
        acc[...] = jnp.zeros_like(acc)

    pieces = [recv_ref[:, r * NB : (r + 1) * NB].reshape(GROUP * NB, BLK) for r in range(PIECES)]
    values = jnp.concatenate(pieces, axis=1)
    lists = [recv_ref[i, PIECES * NB :].astype(F32) for i in range(GROUP)]
    numbers = [rows[:1] * BLK_DEV + rows[1:2] for rows in lists]
    first = lax.broadcasted_iota(jnp.int32, (1, BLK), 1) < NB
    pairs = [jnp.where(first, numbers[i], numbers[i + 1]).astype(jnp.int32) for i in range(0, GROUP, 2)]
    rows = lax.broadcasted_iota(jnp.int32, (MERGED, BLK), 0)
    for m in range(0, BINS, MERGED):
        hot = [jnp.where(rows == pair - m, 1.0, 0.0).astype(BF16) for pair in pairs]
        acc[m : m + MERGED] += dot(jnp.concatenate(hot, axis=1), values)

    @pl.when(step == STEPS - 1)
    def _():
        out_ref[...] = acc[...].astype(BF16)


def merged(received):
    return pl.pallas_call(
        merge_kernel,
        grid=(STEPS,),
        in_specs=[pl.BlockSpec((GROUP, SENT, BLK), lambda s: (s, 0, 0))],
        out_specs=whole(BINS, PIECES * BLK),
        out_shape=jax.ShapeDtypeStruct((BINS, PIECES * BLK), BF16),
        scratch_shapes=[pltpu.VMEM((BINS, PIECES * BLK), F32)],
        compiler_params=pltpu.CompilerParams(vmem_limit_bytes=24 << 20),
        cost_estimate=pl.CostEstimate(
            flops=2 * BINS * OWNERS * NB * PIECES * BLK, bytes_accessed=10 << 20, transcendentals=0
        ),
    )(received)


def add_own(recv_ref, own_ref, flat, total):
    arrived = recv_ref[...].astype(F32).reshape(BINS, PIECES * BLK)
    for r in range(PIECES):
        flat[r * BINS : (r + 1) * BINS] = arrived[:, r * BLK : (r + 1) * BLK]
    for g in range(BLK_DEV):
        for r in range(PIECES):
            rows = slice(r * OWNERS, (r + 1) * OWNERS)
            total[g, rows] = own_ref[g, rows] + flat[pl.ds(r * BINS + g, OWNERS, stride=BLK_DEV)]


def neigh_kernel(recv_ref, own_ref, feat_ref, self_ref, joined_ref, flat, total):
    add_own(recv_ref, own_ref, flat, total)
    neigh = jnp.zeros((D, D), F32)
    for g in range(0, BLK_DEV, 2):
        upper, lower = halves(jnp.concatenate([total[g], total[g + 1]], axis=1))
        feat = feat_ref[g * BLK : (g + 2) * BLK, :]
        neigh += dot(upper, feat) + dot(lower, feat)
    joined_ref[:D] = self_ref[...].astype(BF16)
    joined_ref[D:] = neigh.T.astype(BF16)


VMEM_SPEC = pl.BlockSpec(memory_space=pltpu.VMEM)
TOTAL_SCRATCH = [pltpu.VMEM((PIECES * BINS, BLK), F32), pltpu.VMEM((BLK_DEV, D, BLK), F32)]


def weight_gradients(received, own, features, self_part):
    return pl.pallas_call(
        neigh_kernel,
        in_specs=[VMEM_SPEC] * 4,
        out_specs=VMEM_SPEC,
        out_shape=jax.ShapeDtypeStruct((2 * D, D), BF16),
        scratch_shapes=TOTAL_SCRATCH,
        compiler_params=pltpu.CompilerParams(vmem_limit_bytes=24 << 20),
        cost_estimate=pl.CostEstimate(
            flops=4 * BLK_DEV * BLK * D * D, bytes_accessed=6 << 20, transcendentals=0
        ),
    )(received, own, features, self_part)


def share_kernel(shares_ref, spread_ref):
    share = jnp.sum(shares_ref[...].astype(F32), axis=0, keepdims=True).astype(BF16)
    spread_ref[...] = jnp.broadcast_to(share, spread_ref.shape)


def added_up(shares):
    return pl.pallas_call(
        share_kernel,
        in_specs=[VMEM_SPEC],
        out_specs=VMEM_SPEC,
        out_shape=jax.ShapeDtypeStruct(shares.shape, BF16),
        compiler_params=pltpu.CompilerParams(vmem_limit_bytes=16 << 20),
    )(shares)


def feature_kernel(recv_ref, own_ref, preact_ref, cot_ref, self_ref, neigh_ref, grad_ref, flat, total):
    g = pl.program_id(0)

    @pl.when(g == 0)
    def _():
        add_own(recv_ref, own_ref, flat, total)

    grad = jnp.where(preact_ref[...] > 0, cot_ref[...], 0.0)
    upper, lower = halves(grad)
    w_upper, w_lower = halves(self_ref[...].T)
    result = dot(upper, w_upper) + dot(lower, w_upper) + dot(upper, w_lower)
    upper, lower = halves(jnp.concatenate([total[2 * g], total[2 * g + 1]], axis=1).T)
    w_upper, w_lower = halves(neigh_ref[...].T)
    grad_ref[...] = result + (dot(upper, w_upper) + dot(lower, w_upper) + dot(upper, w_lower))


def feature_gradient(received, own, preact, cotangent, w_self, w_neigh):
    rows = pl.BlockSpec((2 * BLK, D), lambda g: (g, 0))
    return pl.pallas_call(
        feature_kernel,
        grid=(BLK_DEV // 2,),
        in_specs=[
            whole(OWNERS, BLK_DEV, PIECES * BLK),
            whole(BLK_DEV, D, BLK),
            rows,
            rows,
            whole(D, D),
            whole(D, D),
        ],
        out_specs=rows,
        out_shape=jax.ShapeDtypeStruct((BLK_DEV * BLK, D), F32),
        scratch_shapes=TOTAL_SCRATCH,
        compiler_params=pltpu.CompilerParams(vmem_limit_bytes=32 << 20),
        cost_estimate=pl.CostEstimate(
            flops=12 * BLK_DEV * BLK * D * D, bytes_accessed=10 << 20, transcendentals=0
        ),
    )(received, own, preact, cotangent, w_self, w_neigh)


def list_rows(owner, slot):
    lists = jnp.concatenate([owner, slot], axis=0)
    return jnp.pad(jnp.tile(lists, (1, BLK // NB)), ((0, TAG - 2), (0, 0))).astype(BF16)


def shards(features, preact, cotangent, w_self, w_neigh, tile_counts, tile_col, owner, slot):
    own, self_part, outgoing = partials(
        tile_col, tile_counts, preact, cotangent, features, list_rows(owner, slot)
    )
    received = lax.all_to_all(outgoing, "nodes", 0, 0, tiled=True)
    sums = merged(received).reshape(OWNERS, BLK_DEV, PIECES * BLK)
    sums = lax.all_to_all(sums, "nodes", 0, 0, tiled=True)
    joined = weight_gradients(sums, own, features, self_part)

    rows = 2 * D // OWNERS
    shares = lax.all_to_all(joined.reshape(OWNERS, rows, D), "nodes", 0, 0, tiled=True)
    spread, sums = lax.optimization_barrier((added_up(shares), sums))
    both = lax.all_to_all(spread, "nodes", 0, 0, tiled=True).reshape(2 * D, D)
    grad_features = feature_gradient(sums, own, preact, cotangent, w_self, w_neigh)
    scale = 1.0 / math.sqrt(OWNERS * BLK_DEV * BLK)
    return grad_features, both[:D].astype(F32) * scale, both[D:].astype(F32) * scale


def solution(mesh):
    rows = P("nodes", None)
    return jax.shard_map(
        shards,
        mesh=mesh,
        in_specs=(rows, rows, rows, P(), P(), P("nodes", None, None, None), rows, rows, rows),
        out_specs=(rows, P(), P()),
        check_vma=False,
    )
```

```python
import functools
import math

import jax
import jax.numpy as jnp
from jax import lax
from jax.experimental import pallas as pl
from jax.experimental.pallas import tpu as pltpu
from jax.sharding import PartitionSpec as P

D = 512
BLK = 128
BLK_DEV = 8
OWNERS = 128
NB = 64
K = 10
COLUMNS = BLK_DEV + NB
TAG = 16
PIECES = D // OWNERS
SENT = PIECES * NB + TAG
PITCH = BLK + 8
F32 = jnp.float32
BF16 = jnp.bfloat16


def dot(a, b):
    return lax.dot_general(a, b, (((1,), (0,)), ((), ())), preferred_element_type=F32)


def halves(values):
    upper = values.astype(BF16)
    return upper, (values - upper.astype(F32)).astype(BF16)


def whole(*shape):
    return pl.BlockSpec(shape, lambda *_: (0,) * len(shape))


def scatter_kernel(
    col_ref, counts_ref, preact_ref, cot_ref, feat_ref, tag_ref, own_ref, self_ref, send_ref, acc
):
    b = pl.program_id(0)

    @pl.when(b == 0)
    def _():
        acc[...] = jnp.zeros_like(acc)
        self_ref[...] = jnp.zeros_like(self_ref)

    def column(r, c):
        return pl.ds(pl.multiple_of((r * COLUMNS + c) * PITCH, 8), BLK)

    counts = counts_ref[0].astype(F32)
    degree = 1.0 + jnp.sum(jnp.sum(counts, axis=0), axis=1, keepdims=True)
    grad = jnp.where(preact_ref[...] > 0, cot_ref[...], 0.0)
    feat = feat_ref[...].astype(F32).T.astype(BF16)
    self_ref[...] += dot(jnp.concatenate([feat, feat], axis=1), jnp.concatenate(halves(grad), axis=0))
    both = jnp.concatenate(halves(grad / jnp.sqrt(degree)), axis=0)
    for t in range(0, K, 2):
        pair = jnp.concatenate([counts[t].T, counts[t + 1].T], axis=0).astype(BF16)
        part = dot(jnp.concatenate([pair, pair], axis=1), both)
        for i in range(2):
            for r in range(PIECES):
                acc[column(r, col_ref[b, t + i])] += part[i * BLK : (i + 1) * BLK, r * BLK : (r + 1) * BLK]

    @pl.when(b == BLK_DEV - 1)
    def _():
        @pl.loop(0, OWNERS)
        def _(j):
            for r in range(PIECES):
                start = (r * COLUMNS + BLK_DEV) * PITCH + j
                send_ref[j, r * NB : (r + 1) * NB] = acc[pl.ds(start, NB, stride=PITCH)].astype(BF16)
            send_ref[j, PIECES * NB :] = tag_ref[...]

        for c in range(BLK_DEV):
            for r in range(PIECES):
                own_ref[c * BLK : (c + 1) * BLK, r * BLK : (r + 1) * BLK] = acc[column(r, c)]


def partials(tile_col, counts, preact, cotangent, features, tag):
    rows = pl.BlockSpec((BLK, D), lambda b, *_: (b, 0))
    return pl.pallas_call(
        scatter_kernel,
        grid_spec=pltpu.PrefetchScalarGridSpec(
            num_scalar_prefetch=1,
            grid=(BLK_DEV,),
            in_specs=[
                pl.BlockSpec((1, K, BLK, BLK), lambda b, *_: (b, 0, 0, 0)),
                rows,
                rows,
                rows,
                whole(TAG, BLK),
            ],
            out_specs=[whole(BLK_DEV * BLK, D), whole(D, D), pl.BlockSpec(memory_space=pltpu.VMEM)],
            scratch_shapes=[
                pltpu.VMEM((PIECES * COLUMNS * PITCH, BLK), F32),
            ],
        ),
        out_shape=[
            pltpu.VMEM((BLK_DEV * BLK, D), F32),
            pltpu.VMEM((D, D), F32),
            pltpu.VMEM((OWNERS, SENT, BLK), BF16),
        ],
        compiler_params=pltpu.CompilerParams(vmem_limit_bytes=50 << 20),
        cost_estimate=pl.CostEstimate(
            flops=4 * BLK_DEV * K * BLK * BLK * D, bytes_accessed=22 << 20, transcendentals=0
        ),
    )(tile_col, counts, preact, cotangent, features, tag)


GROUP = 32
STEPS = OWNERS // GROUP
BINS = OWNERS * BLK_DEV
MERGED = 256


def merge_kernel(recv_ref, out_ref, acc):
    step = pl.program_id(0)

    @pl.when(step == 0)
    def _():
        acc[...] = jnp.zeros_like(acc)

    pieces = [recv_ref[:, r * NB : (r + 1) * NB].reshape(GROUP * NB, BLK) for r in range(PIECES)]
    values = jnp.concatenate(pieces, axis=1)
    lists = [recv_ref[i, PIECES * NB :].astype(F32) for i in range(GROUP)]
    numbers = [rows[:1] * BLK_DEV + rows[1:2] for rows in lists]
    first = lax.broadcasted_iota(jnp.int32, (1, BLK), 1) < NB
    pairs = [jnp.where(first, numbers[i], numbers[i + 1]).astype(jnp.int32) for i in range(0, GROUP, 2)]
    rows = lax.broadcasted_iota(jnp.int32, (MERGED, BLK), 0)
    for m in range(0, BINS, MERGED):
        hot = [jnp.where(rows == pair - m, 1.0, 0.0).astype(BF16) for pair in pairs]
        acc[m : m + MERGED] += dot(jnp.concatenate(hot, axis=1), values)

    @pl.when(step == STEPS - 1)
    def _():
        out_ref[...] = acc[...].astype(BF16)


def merged(received):
    return pl.pallas_call(
        merge_kernel,
        grid=(STEPS,),
        in_specs=[pl.BlockSpec((GROUP, SENT, BLK), lambda s: (s, 0, 0))],
        out_specs=whole(BINS, PIECES * BLK),
        out_shape=jax.ShapeDtypeStruct((BINS, PIECES * BLK), BF16),
        scratch_shapes=[pltpu.VMEM((BINS, PIECES * BLK), F32)],
        compiler_params=pltpu.CompilerParams(vmem_limit_bytes=24 << 20),
        cost_estimate=pl.CostEstimate(
            flops=2 * BINS * OWNERS * NB * PIECES * BLK, bytes_accessed=10 << 20, transcendentals=0
        ),
    )(received)


def add_own(recv_ref, own_ref, flat, total):
    arrived = recv_ref[...].astype(F32).reshape(BINS, D)
    for r in range(PIECES):
        flat[r * BINS : (r + 1) * BINS] = arrived[:, r * BLK : (r + 1) * BLK]
    for g in range(BLK_DEV):
        for r in range(PIECES):
            place = slice(g * BLK, (g + 1) * BLK), slice(r * BLK, (r + 1) * BLK)
            total[place] = own_ref[place] + flat[pl.ds(r * BINS + g, OWNERS, stride=BLK_DEV)]


def neigh_kernel(recv_ref, own_ref, feat_ref, self_ref, joined_ref, flat, total):
    add_own(recv_ref, own_ref, flat, total)
    neigh = jnp.zeros((D, D), F32)
    for g in range(0, BLK_DEV * BLK, 2 * BLK):
        upper, lower = halves(total[g : g + 2 * BLK])
        feat = feat_ref[g : g + 2 * BLK].astype(F32).T.astype(BF16)
        neigh += dot(feat, upper) + dot(feat, lower)
    joined_ref[:D] = self_ref[...].astype(BF16)
    joined_ref[D:] = neigh.astype(BF16)


VMEM_SPEC = pl.BlockSpec(memory_space=pltpu.VMEM)
TOTAL_SCRATCH = [pltpu.VMEM((PIECES * BINS, BLK), F32), pltpu.VMEM((BLK_DEV * BLK, D), F32)]


def weight_gradients(received, own, features, self_part):
    return pl.pallas_call(
        neigh_kernel,
        in_specs=[VMEM_SPEC] * 4,
        out_specs=VMEM_SPEC,
        out_shape=jax.ShapeDtypeStruct((2 * D, D), BF16),
        scratch_shapes=TOTAL_SCRATCH,
        compiler_params=pltpu.CompilerParams(vmem_limit_bytes=24 << 20),
        cost_estimate=pl.CostEstimate(
            flops=4 * BLK_DEV * BLK * D * D, bytes_accessed=6 << 20, transcendentals=0
        ),
    )(received, own, features, self_part)


def share_kernel(shares_ref, spread_ref):
    share = jnp.sum(shares_ref[...].astype(F32), axis=0, keepdims=True).astype(BF16)
    spread_ref[...] = jnp.broadcast_to(share, spread_ref.shape)


def added_up(shares):
    return pl.pallas_call(
        share_kernel,
        in_specs=[VMEM_SPEC],
        out_specs=VMEM_SPEC,
        out_shape=jax.ShapeDtypeStruct(shares.shape, BF16),
        compiler_params=pltpu.CompilerParams(vmem_limit_bytes=16 << 20),
    )(shares)


def feature_kernel(recv_ref, own_ref, preact_ref, cot_ref, self_ref, neigh_ref, grad_ref, flat, total):
    g = pl.program_id(0)

    @pl.when(g == 0)
    def _():
        add_own(recv_ref, own_ref, flat, total)

    grad = jnp.where(preact_ref[...] > 0, cot_ref[...], 0.0)
    upper, lower = halves(grad)
    w_upper, w_lower = halves(self_ref[...].T)
    result = dot(upper, w_upper) + dot(lower, w_upper) + dot(upper, w_lower)
    upper, lower = halves(total[pl.ds(pl.multiple_of(2 * BLK * g, BLK), 2 * BLK)])
    w_upper, w_lower = halves(neigh_ref[...].T)
    grad_ref[...] = result + (dot(upper, w_upper) + dot(lower, w_upper) + dot(upper, w_lower))


def feature_gradient(received, own, preact, cotangent, w_self, w_neigh):
    rows = pl.BlockSpec((2 * BLK, D), lambda g: (g, 0))
    return pl.pallas_call(
        feature_kernel,
        grid=(BLK_DEV // 2,),
        in_specs=[
            whole(OWNERS, BLK_DEV, PIECES * BLK),
            whole(BLK_DEV * BLK, D),
            rows,
            rows,
            whole(D, D),
            whole(D, D),
        ],
        out_specs=rows,
        out_shape=jax.ShapeDtypeStruct((BLK_DEV * BLK, D), F32),
        scratch_shapes=TOTAL_SCRATCH,
        compiler_params=pltpu.CompilerParams(vmem_limit_bytes=20 << 20),
        cost_estimate=pl.CostEstimate(
            flops=12 * BLK_DEV * BLK * D * D, bytes_accessed=10 << 20, transcendentals=0
        ),
    )(received, own, preact, cotangent, w_self, w_neigh)


def list_rows(owner, slot):
    lists = jnp.concatenate([owner, slot], axis=0)
    return jnp.pad(jnp.tile(lists, (1, BLK // NB)), ((0, TAG - 2), (0, 0))).astype(BF16)


def shards(features, preact, cotangent, w_self, w_neigh, tile_counts, tile_col, owner, slot):
    own, self_part, outgoing = partials(
        tile_col, tile_counts, preact, cotangent, features, list_rows(owner, slot)
    )
    received = lax.all_to_all(outgoing, "nodes", 0, 0, tiled=True)
    sums = merged(received).reshape(OWNERS, BLK_DEV, PIECES * BLK)
    sums = lax.all_to_all(sums, "nodes", 0, 0, tiled=True)
    joined = weight_gradients(sums, own, features, self_part)

    rows = 2 * D // OWNERS
    shares = lax.all_to_all(joined.reshape(OWNERS, rows, D), "nodes", 0, 0, tiled=True)
    spread, sums = lax.optimization_barrier((added_up(shares), sums))
    both = lax.all_to_all(spread, "nodes", 0, 0, tiled=True).reshape(2 * D, D)
    grad_features = feature_gradient(sums, own, preact, cotangent, w_self, w_neigh)
    scale = 1.0 / math.sqrt(OWNERS * BLK_DEV * BLK)
    return grad_features, both[:D].astype(F32) * scale, both[D:].astype(F32) * scale


def solution(mesh):
    rows = P("nodes", None)
    return jax.shard_map(
        shards,
        mesh=mesh,
        in_specs=(rows, rows, rows, P(), P(), P("nodes", None, None, None), rows, rows, rows),
        out_specs=(rows, P(), P()),
        check_vma=False,
    )
```

```python
import functools
import math

import jax
import jax.numpy as jnp
from jax import lax
from jax.experimental import pallas as pl
from jax.experimental.pallas import tpu as pltpu
from jax.sharding import PartitionSpec as P

D = 512
BLK = 128
BLK_DEV = 8
OWNERS = 128
NB = 64
K = 10
COLUMNS = BLK_DEV + NB
TAG = 16
PIECES = D // OWNERS
SENT = PIECES * NB + TAG
PITCH = BLK + 8
F32 = jnp.float32
BF16 = jnp.bfloat16


def dot(a, b):
    return lax.dot_general(a, b, (((1,), (0,)), ((), ())), preferred_element_type=F32)


def halves(values):
    upper = values.astype(BF16)
    return upper, (values - upper.astype(F32)).astype(BF16)


def whole(*shape):
    return pl.BlockSpec(shape, lambda *_: (0,) * len(shape))


def scatter_kernel(
    col_ref, counts_ref, preact_ref, cot_ref, feat_ref, tag_ref, own_ref, self_ref, send_ref, acc
):
    b = pl.program_id(0)

    @pl.when(b == 0)
    def _():
        acc[...] = jnp.zeros_like(acc)
        self_ref[...] = jnp.zeros_like(self_ref)

    def column(r, c):
        return pl.ds(pl.multiple_of((r * COLUMNS + c) * PITCH, 8), BLK)

    counts = counts_ref[0].astype(F32)
    degree = 1.0 + jnp.sum(jnp.sum(counts, axis=0), axis=1, keepdims=True)
    grad = jnp.where(preact_ref[...] > 0, cot_ref[...], 0.0)
    feat = feat_ref[...].astype(F32).T.astype(BF16)
    self_ref[...] += dot(jnp.concatenate([feat, feat], axis=1), jnp.concatenate(halves(grad), axis=0))
    both = jnp.concatenate(halves(grad / jnp.sqrt(degree)), axis=0)
    for t in range(0, K, 2):
        pair = jnp.concatenate([counts[t].T, counts[t + 1].T], axis=0).astype(BF16)
        part = dot(jnp.concatenate([pair, pair], axis=1), both)
        for i in range(2):
            for r in range(PIECES):
                acc[column(r, col_ref[b, t + i])] += part[i * BLK : (i + 1) * BLK, r * BLK : (r + 1) * BLK]

    @pl.when(b == BLK_DEV - 1)
    def _():
        @pl.loop(0, OWNERS)
        def _(j):
            for r in range(PIECES):
                start = (r * COLUMNS + BLK_DEV) * PITCH + j
                send_ref[j, r * NB : (r + 1) * NB] = acc[pl.ds(start, NB, stride=PITCH)].astype(BF16)
            send_ref[j, PIECES * NB :] = tag_ref[...]

        for c in range(BLK_DEV):
            for r in range(PIECES):
                own_ref[c * BLK : (c + 1) * BLK, r * BLK : (r + 1) * BLK] = acc[column(r, c)]


def partials(tile_col, counts, preact, cotangent, features, tag):
    rows = pl.BlockSpec((BLK, D), lambda b, *_: (b, 0))
    return pl.pallas_call(
        scatter_kernel,
        grid_spec=pltpu.PrefetchScalarGridSpec(
            num_scalar_prefetch=1,
            grid=(BLK_DEV,),
            in_specs=[
                pl.BlockSpec((1, K, BLK, BLK), lambda b, *_: (b, 0, 0, 0)),
                rows,
                rows,
                rows,
                whole(TAG, BLK),
            ],
            out_specs=[whole(BLK_DEV * BLK, D), whole(D, D), pl.BlockSpec(memory_space=pltpu.VMEM)],
            scratch_shapes=[
                pltpu.VMEM((PIECES * COLUMNS * PITCH, BLK), F32),
            ],
        ),
        out_shape=[
            pltpu.VMEM((BLK_DEV * BLK, D), F32),
            pltpu.VMEM((D, D), F32),
            pltpu.VMEM((OWNERS, SENT, BLK), BF16),
        ],
        compiler_params=pltpu.CompilerParams(vmem_limit_bytes=50 << 20),
        cost_estimate=pl.CostEstimate(
            flops=4 * BLK_DEV * K * BLK * BLK * D, bytes_accessed=22 << 20, transcendentals=0
        ),
    )(tile_col, counts, preact, cotangent, features, tag)


GROUP = 32
STEPS = OWNERS // GROUP
BINS = OWNERS * BLK_DEV
MERGED = 256


def merge_kernel(recv_ref, out_ref, acc):
    step = pl.program_id(0)

    @pl.when(step == 0)
    def _():
        acc[...] = jnp.zeros_like(acc)

    pieces = [recv_ref[:, r * NB : (r + 1) * NB].reshape(GROUP * NB, BLK) for r in range(PIECES)]
    values = jnp.concatenate(pieces, axis=1)
    lists = [recv_ref[i, PIECES * NB :].astype(F32) for i in range(GROUP)]
    numbers = [rows[:1] * BLK_DEV + rows[1:2] for rows in lists]
    first = lax.broadcasted_iota(jnp.int32, (1, BLK), 1) < NB
    pairs = [jnp.where(first, numbers[i], numbers[i + 1]).astype(jnp.int32) for i in range(0, GROUP, 2)]
    rows = lax.broadcasted_iota(jnp.int32, (MERGED, BLK), 0)
    for m in range(0, BINS, MERGED):
        hot = [jnp.where(rows == pair - m, 1.0, 0.0).astype(BF16) for pair in pairs]
        acc[m : m + MERGED] += dot(jnp.concatenate(hot, axis=1), values)

    @pl.when(step == STEPS - 1)
    def _():
        out_ref[...] = acc[...].astype(BF16)


def merged(received):
    return pl.pallas_call(
        merge_kernel,
        grid=(STEPS,),
        in_specs=[pl.BlockSpec((GROUP, SENT, BLK), lambda s: (s, 0, 0))],
        out_specs=whole(BINS, PIECES * BLK),
        out_shape=jax.ShapeDtypeStruct((BINS, PIECES * BLK), BF16),
        scratch_shapes=[pltpu.VMEM((BINS, PIECES * BLK), F32)],
        compiler_params=pltpu.CompilerParams(vmem_limit_bytes=24 << 20),
        cost_estimate=pl.CostEstimate(
            flops=2 * BINS * OWNERS * NB * PIECES * BLK, bytes_accessed=10 << 20, transcendentals=0
        ),
    )(received)


def add_own(recv_ref, own_ref, flat, total):
    arrived = recv_ref[...].astype(F32).reshape(BINS, D)
    for r in range(PIECES):
        flat[r * BINS : (r + 1) * BINS] = arrived[:, r * BLK : (r + 1) * BLK]
    for g in range(BLK_DEV):
        for r in range(PIECES):
            place = slice(g * BLK, (g + 1) * BLK), slice(r * BLK, (r + 1) * BLK)
            total[place] = own_ref[place] + flat[pl.ds(r * BINS + g, OWNERS, stride=BLK_DEV)]


def neigh_kernel(recv_ref, own_ref, feat_ref, self_ref, joined_ref, flat, total):
    add_own(recv_ref, own_ref, flat, total)
    neigh = jnp.zeros((D, D), F32)
    for g in range(0, BLK_DEV * BLK, 2 * BLK):
        upper, lower = halves(total[g : g + 2 * BLK])
        feat = feat_ref[g : g + 2 * BLK].astype(F32).T.astype(BF16)
        neigh += dot(feat, upper) + dot(feat, lower)
    joined_ref[:D] = self_ref[...].astype(BF16)
    joined_ref[D:] = neigh.astype(BF16)


VMEM_SPEC = pl.BlockSpec(memory_space=pltpu.VMEM)
TOTAL_SCRATCH = [pltpu.VMEM((PIECES * BINS, BLK), F32), pltpu.VMEM((BLK_DEV * BLK, D), F32)]


def weight_gradients(received, own, features, self_part):
    return pl.pallas_call(
        neigh_kernel,
        in_specs=[VMEM_SPEC] * 4,
        out_specs=VMEM_SPEC,
        out_shape=jax.ShapeDtypeStruct((2 * D, D), BF16),
        scratch_shapes=TOTAL_SCRATCH,
        compiler_params=pltpu.CompilerParams(vmem_limit_bytes=24 << 20),
        cost_estimate=pl.CostEstimate(
            flops=4 * BLK_DEV * BLK * D * D, bytes_accessed=6 << 20, transcendentals=0
        ),
    )(received, own, features, self_part)


def share_kernel(shares_ref, spread_ref):
    share = jnp.sum(shares_ref[...].astype(F32), axis=0, keepdims=True).astype(BF16)
    spread_ref[...] = jnp.broadcast_to(share, spread_ref.shape)


def added_up(shares):
    return pl.pallas_call(
        share_kernel,
        in_specs=[VMEM_SPEC],
        out_specs=VMEM_SPEC,
        out_shape=jax.ShapeDtypeStruct(shares.shape, BF16),
        compiler_params=pltpu.CompilerParams(vmem_limit_bytes=16 << 20),
    )(shares)


def feature_kernel(recv_ref, own_ref, preact_ref, cot_ref, self_ref, neigh_ref, grad_ref, flat, total):
    g = pl.program_id(0)

    @pl.when(g == 0)
    def _():
        add_own(recv_ref, own_ref, flat, total)

    grad = jnp.where(preact_ref[...] > 0, cot_ref[...], 0.0)
    upper, lower = halves(grad)
    w_upper, w_lower = halves(self_ref[...].T)
    result = dot(upper, w_upper) + dot(lower, w_upper) + dot(upper, w_lower)
    upper, lower = halves(total[pl.ds(pl.multiple_of(2 * BLK * g, BLK), 2 * BLK)])
    w_upper, w_lower = halves(neigh_ref[...].T)
    grad_ref[...] = result + (dot(upper, w_upper) + dot(lower, w_upper) + dot(upper, w_lower))


def feature_gradient(received, own, preact, cotangent, w_self, w_neigh):
    rows = pl.BlockSpec((2 * BLK, D), lambda g: (g, 0))
    return pl.pallas_call(
        feature_kernel,
        grid=(BLK_DEV // 2,),
        in_specs=[
            whole(OWNERS, BLK_DEV, PIECES * BLK),
            whole(BLK_DEV * BLK, D),
            rows,
            rows,
            whole(D, D),
            whole(D, D),
        ],
        out_specs=rows,
        out_shape=jax.ShapeDtypeStruct((BLK_DEV * BLK, D), F32),
        scratch_shapes=TOTAL_SCRATCH,
        compiler_params=pltpu.CompilerParams(vmem_limit_bytes=20 << 20),
        cost_estimate=pl.CostEstimate(
            flops=12 * BLK_DEV * BLK * D * D, bytes_accessed=10 << 20, transcendentals=0
        ),
    )(received, own, preact, cotangent, w_self, w_neigh)


def list_rows(owner, slot):
    lists = jnp.concatenate([owner, slot], axis=0)
    return jnp.pad(jnp.tile(lists, (1, BLK // NB)), ((0, TAG - 2), (0, 0))).astype(BF16)


def shards(features, preact, cotangent, w_self, w_neigh, tile_counts, tile_col, owner, slot):
    own, self_part, outgoing = partials(
        tile_col, tile_counts, preact, cotangent, features, list_rows(owner, slot)
    )
    received = lax.all_to_all(outgoing, "nodes", 0, 0, tiled=True)
    sums = merged(received).reshape(OWNERS, BLK_DEV, PIECES * BLK)
    sums = lax.all_to_all(sums, "nodes", 0, 0, tiled=True)
    joined = weight_gradients(sums, own, features, self_part)

    joined, sums = lax.optimization_barrier((joined, sums))
    rows = 2 * D // OWNERS
    shares = lax.all_to_all(joined.reshape(OWNERS, rows, D), "nodes", 0, 0, tiled=True)
    grad_features = feature_gradient(sums, own, preact, cotangent, w_self, w_neigh)
    spread, grad_features = lax.optimization_barrier((added_up(shares), grad_features))
    both = lax.all_to_all(spread, "nodes", 0, 0, tiled=True).reshape(2 * D, D)
    scale = 1.0 / math.sqrt(OWNERS * BLK_DEV * BLK)
    return grad_features, both[:D].astype(F32) * scale, both[D:].astype(F32) * scale


def solution(mesh):
    rows = P("nodes", None)
    return jax.shard_map(
        shards,
        mesh=mesh,
        in_specs=(rows, rows, rows, P(), P(), P("nodes", None, None, None), rows, rows, rows),
        out_specs=(rows, P(), P()),
        check_vma=False,
    )
```

```python
import functools
import math

import jax
import jax.numpy as jnp
from jax import lax
from jax.experimental import pallas as pl
from jax.experimental.pallas import tpu as pltpu
from jax.sharding import PartitionSpec as P

D = 512
BLK = 128
BLK_DEV = 8
OWNERS = 128
NB = 64
K = 10
COLUMNS = BLK_DEV + NB
TAG = 16
PIECES = D // OWNERS
SENT = PIECES * NB + TAG
PITCH = BLK + 8
F32 = jnp.float32
BF16 = jnp.bfloat16


def dot(a, b):
    return lax.dot_general(a, b, (((1,), (0,)), ((), ())), preferred_element_type=F32)


def halves(values):
    upper = values.astype(BF16)
    return upper, (values - upper.astype(F32)).astype(BF16)


def whole(*shape):
    return pl.BlockSpec(shape, lambda *_: (0,) * len(shape))


def scatter_kernel(
    col_ref, counts_ref, preact_ref, cot_ref, feat_ref, owner_ref, slot_ref, own_ref, self_ref, send_ref, acc, seen
):
    b = pl.program_id(0)

    @pl.when(b == 0)
    def _():
        for r in range(PIECES):
            acc[pl.ds(r * COLUMNS * PITCH, BLK_DEV * PITCH)] = jnp.zeros((BLK_DEV * PITCH, BLK), F32)
        self_ref[...] = jnp.zeros_like(self_ref)

        @pl.loop(0, COLUMNS)
        def _(c):
            seen[c] = jnp.where(c < BLK_DEV, 1, 0)

    def column(r, c):
        return pl.ds(pl.multiple_of((r * COLUMNS + c) * PITCH, 8), BLK)

    counts = counts_ref[0].astype(F32)
    degree = 1.0 + jnp.sum(jnp.sum(counts, axis=0), axis=1, keepdims=True)
    grad = jnp.where(preact_ref[...] > 0, cot_ref[...], 0.0)
    feat = feat_ref[...].astype(F32).T.astype(BF16)
    self_ref[...] += dot(jnp.concatenate([feat, feat], axis=1), jnp.concatenate(halves(grad), axis=0))
    both = jnp.concatenate(halves(grad / jnp.sqrt(degree)), axis=0)
    for t in range(0, K, 2):
        pair = jnp.concatenate([counts[t].T, counts[t + 1].T], axis=0).astype(BF16)
        part = dot(jnp.concatenate([pair, pair], axis=1), both)
        for i in range(2):
            c = col_ref[b, t + i]
            started = seen[c] > 0
            seen[c] = 1
            for r in range(PIECES):
                place = column(r, c)
                new = part[i * BLK : (i + 1) * BLK, r * BLK : (r + 1) * BLK]
                acc[place] = jnp.where(started, acc[place], 0.0) + new

    @pl.when(b == BLK_DEV - 1)
    def _():
        row = lax.broadcasted_iota(jnp.int32, (TAG, BLK), 0)
        owners, slots = (jnp.concatenate([ref[...]] * 2, axis=1) for ref in (owner_ref, slot_ref))
        tag = jnp.where(row == 0, owners, jnp.where(row == 1, slots, 0)).astype(F32).astype(BF16)

        @pl.loop(0, OWNERS)
        def _(j):
            for r in range(PIECES):
                start = (r * COLUMNS + BLK_DEV) * PITCH + j
                send_ref[j, r * NB : (r + 1) * NB] = acc[pl.ds(start, NB, stride=PITCH)].astype(BF16)
            send_ref[j, PIECES * NB :] = tag

        for c in range(BLK_DEV):
            for r in range(PIECES):
                own_ref[c * BLK : (c + 1) * BLK, r * BLK : (r + 1) * BLK] = acc[column(r, c)]


def partials(tile_col, counts, preact, cotangent, features, owner, slot):
    rows = pl.BlockSpec((BLK, D), lambda b, *_: (b, 0))
    return pl.pallas_call(
        scatter_kernel,
        grid_spec=pltpu.PrefetchScalarGridSpec(
            num_scalar_prefetch=1,
            grid=(BLK_DEV,),
            in_specs=[
                pl.BlockSpec((1, K, BLK, BLK), lambda b, *_: (b, 0, 0, 0)),
                rows,
                rows,
                rows,
                whole(1, NB),
                whole(1, NB),
            ],
            out_specs=[whole(BLK_DEV * BLK, D), whole(D, D), pl.BlockSpec(memory_space=pltpu.VMEM)],
            scratch_shapes=[
                pltpu.VMEM(((PIECES * COLUMNS + 1) * PITCH, BLK), F32),
                pltpu.SMEM((COLUMNS,), jnp.int32),
            ],
        ),
        out_shape=[
            pltpu.VMEM((BLK_DEV * BLK, D), F32),
            pltpu.VMEM((D, D), F32),
            pltpu.VMEM((OWNERS, SENT, BLK), BF16),
        ],
        compiler_params=pltpu.CompilerParams(vmem_limit_bytes=50 << 20),
        cost_estimate=pl.CostEstimate(
            flops=4 * BLK_DEV * K * BLK * BLK * D, bytes_accessed=22 << 20, transcendentals=0
        ),
    )(tile_col, counts, preact, cotangent, features, owner, slot)


GROUP = 32
STEPS = OWNERS // GROUP
BINS = OWNERS * BLK_DEV
MERGED = 256


def merge_kernel(recv_ref, out_ref, acc):
    step = pl.program_id(0)

    @pl.when(step == 0)
    def _():
        acc[...] = jnp.zeros_like(acc)

    pieces = [recv_ref[:, r * NB : (r + 1) * NB].reshape(GROUP * NB, BLK) for r in range(PIECES)]
    values = jnp.concatenate(pieces, axis=1)
    lists = [recv_ref[i, PIECES * NB :].astype(F32) for i in range(GROUP)]
    numbers = [rows[:1] * BLK_DEV + rows[1:2] for rows in lists]
    first = lax.broadcasted_iota(jnp.int32, (1, BLK), 1) < NB
    pairs = [jnp.where(first, numbers[i], numbers[i + 1]).astype(jnp.int32) for i in range(0, GROUP, 2)]
    rows = lax.broadcasted_iota(jnp.int32, (MERGED, BLK), 0)
    for m in range(0, BINS, MERGED):
        hot = [jnp.where(rows == pair - m, 1.0, 0.0).astype(BF16) for pair in pairs]
        acc[m : m + MERGED] += dot(jnp.concatenate(hot, axis=1), values)

    @pl.when(step == STEPS - 1)
    def _():
        out_ref[...] = acc[...].astype(BF16)


def merged(received):
    return pl.pallas_call(
        merge_kernel,
        grid=(STEPS,),
        in_specs=[pl.BlockSpec((GROUP, SENT, BLK), lambda s: (s, 0, 0))],
        out_specs=whole(BINS, PIECES * BLK),
        out_shape=jax.ShapeDtypeStruct((BINS, PIECES * BLK), BF16),
        scratch_shapes=[pltpu.VMEM((BINS, PIECES * BLK), F32)],
        compiler_params=pltpu.CompilerParams(vmem_limit_bytes=24 << 20),
        cost_estimate=pl.CostEstimate(
            flops=2 * BINS * OWNERS * NB * PIECES * BLK, bytes_accessed=10 << 20, transcendentals=0
        ),
    )(received)


def add_own(recv_ref, own_ref, flat, total):
    arrived = recv_ref[...].astype(F32).reshape(BINS, D)
    for r in range(PIECES):
        flat[r * BINS : (r + 1) * BINS] = arrived[:, r * BLK : (r + 1) * BLK]
    for g in range(BLK_DEV):
        for r in range(PIECES):
            place = slice(g * BLK, (g + 1) * BLK), slice(r * BLK, (r + 1) * BLK)
            total[place] = own_ref[place] + flat[pl.ds(r * BINS + g, OWNERS, stride=BLK_DEV)]


def neigh_kernel(recv_ref, own_ref, feat_ref, self_ref, joined_ref, flat, total):
    add_own(recv_ref, own_ref, flat, total)
    neigh = jnp.zeros((D, D), F32)
    for g in range(0, BLK_DEV * BLK, 2 * BLK):
        upper, lower = halves(total[g : g + 2 * BLK])
        feat = feat_ref[g : g + 2 * BLK].astype(F32).T.astype(BF16)
        neigh += dot(feat, upper) + dot(feat, lower)
    joined_ref[:D] = self_ref[...].astype(BF16)
    joined_ref[D:] = neigh.astype(BF16)


VMEM_SPEC = pl.BlockSpec(memory_space=pltpu.VMEM)
TOTAL_SCRATCH = [pltpu.VMEM((PIECES * BINS + BLK_DEV, BLK), F32), pltpu.VMEM((BLK_DEV * BLK, D), F32)]


def weight_gradients(received, own, features, self_part):
    return pl.pallas_call(
        neigh_kernel,
        in_specs=[VMEM_SPEC] * 4,
        out_specs=VMEM_SPEC,
        out_shape=jax.ShapeDtypeStruct((2 * D, D), BF16),
        scratch_shapes=TOTAL_SCRATCH,
        compiler_params=pltpu.CompilerParams(vmem_limit_bytes=24 << 20),
        cost_estimate=pl.CostEstimate(
            flops=4 * BLK_DEV * BLK * D * D, bytes_accessed=6 << 20, transcendentals=0
        ),
    )(received, own, features, self_part)


def share_kernel(shares_ref, spread_ref):
    share = jnp.sum(shares_ref[...].astype(F32), axis=0, keepdims=True).astype(BF16)
    spread_ref[...] = jnp.broadcast_to(share, spread_ref.shape)


def added_up(shares):
    return pl.pallas_call(
        share_kernel,
        in_specs=[VMEM_SPEC],
        out_specs=VMEM_SPEC,
        out_shape=jax.ShapeDtypeStruct(shares.shape, BF16),
        compiler_params=pltpu.CompilerParams(vmem_limit_bytes=16 << 20),
    )(shares)


def feature_kernel(recv_ref, own_ref, preact_ref, cot_ref, self_ref, neigh_ref, grad_ref, flat, total):
    g = pl.program_id(0)

    @pl.when(g == 0)
    def _():
        add_own(recv_ref, own_ref, flat, total)

    grad = jnp.where(preact_ref[...] > 0, cot_ref[...], 0.0)
    upper, lower = halves(grad)
    w_upper, w_lower = halves(self_ref[...].T)
    result = dot(upper, w_upper) + dot(lower, w_upper) + dot(upper, w_lower)
    upper, lower = halves(total[pl.ds(pl.multiple_of(2 * BLK * g, BLK), 2 * BLK)])
    w_upper, w_lower = halves(neigh_ref[...].T)
    grad_ref[...] = result + (dot(upper, w_upper) + dot(lower, w_upper) + dot(upper, w_lower))


def feature_gradient(received, own, preact, cotangent, w_self, w_neigh):
    rows = pl.BlockSpec((2 * BLK, D), lambda g: (g, 0))
    return pl.pallas_call(
        feature_kernel,
        grid=(BLK_DEV // 2,),
        in_specs=[
            whole(OWNERS, BLK_DEV, PIECES * BLK),
            whole(BLK_DEV * BLK, D),
            rows,
            rows,
            whole(D, D),
            whole(D, D),
        ],
        out_specs=rows,
        out_shape=jax.ShapeDtypeStruct((BLK_DEV * BLK, D), F32),
        scratch_shapes=TOTAL_SCRATCH,
        compiler_params=pltpu.CompilerParams(vmem_limit_bytes=20 << 20),
        cost_estimate=pl.CostEstimate(
            flops=12 * BLK_DEV * BLK * D * D, bytes_accessed=10 << 20, transcendentals=0
        ),
    )(received, own, preact, cotangent, w_self, w_neigh)


def shards(features, preact, cotangent, w_self, w_neigh, tile_counts, tile_col, owner, slot):
    own, self_part, outgoing = partials(tile_col, tile_counts, preact, cotangent, features, owner, slot)
    received = lax.all_to_all(outgoing, "nodes", 0, 0, tiled=True)
    sums = merged(received).reshape(OWNERS, BLK_DEV, PIECES * BLK)
    sums = lax.all_to_all(sums, "nodes", 0, 0, tiled=True)
    joined = weight_gradients(sums, own, features, self_part)

    joined, sums = lax.optimization_barrier((joined, sums))
    rows = 2 * D // OWNERS
    shares = lax.all_to_all(joined.reshape(OWNERS, rows, D), "nodes", 0, 0, tiled=True)
    grad_features = feature_gradient(sums, own, preact, cotangent, w_self, w_neigh)
    spread, grad_features = lax.optimization_barrier((added_up(shares), grad_features))
    both = lax.all_to_all(spread, "nodes", 0, 0, tiled=True).reshape(2 * D, D)
    scale = 1.0 / math.sqrt(OWNERS * BLK_DEV * BLK)
    return grad_features, both[:D].astype(F32) * scale, both[D:].astype(F32) * scale


def solution(mesh):
    rows = P("nodes", None)
    return jax.shard_map(
        shards,
        mesh=mesh,
        in_specs=(rows, rows, rows, P(), P(), P("nodes", None, None, None), rows, rows, rows),
        out_specs=(rows, P(), P()),
        check_vma=False,
    )
```

```python
import functools
import math

import jax
import jax.numpy as jnp
from jax import lax
from jax.experimental import pallas as pl
from jax.experimental.pallas import tpu as pltpu
from jax.sharding import PartitionSpec as P

D = 512
BLK = 128
BLK_DEV = 8
OWNERS = 128
NB = 64
K = 10
COLUMNS = BLK_DEV + NB
TAG = 16
PIECES = D // OWNERS
SENT = PIECES * NB + TAG
PITCH = BLK + 8
F32 = jnp.float32
BF16 = jnp.bfloat16


def dot(a, b):
    return lax.dot_general(a, b, (((1,), (0,)), ((), ())), preferred_element_type=F32)


def halves(values):
    upper = values.astype(BF16)
    return upper, (values - upper.astype(F32)).astype(BF16)


def whole(*shape):
    return pl.BlockSpec(shape, lambda *_: (0,) * len(shape))


def scatter_kernel(
    col_ref, counts_ref, preact_ref, cot_ref, feat_ref, owner_ref, slot_ref, own_ref, self_ref, send_ref, acc, seen
):
    b = pl.program_id(0)

    @pl.when(b == 0)
    def _():
        for r in range(PIECES):
            acc[pl.ds(r * COLUMNS * PITCH, BLK_DEV * PITCH)] = jnp.zeros((BLK_DEV * PITCH, BLK), F32)
        self_ref[...] = jnp.zeros_like(self_ref)

        @pl.loop(0, COLUMNS)
        def _(c):
            seen[c] = jnp.where(c < BLK_DEV, 1, 0)

    def column(r, c):
        return pl.ds(pl.multiple_of((r * COLUMNS + c) * PITCH, 8), BLK)

    counts = counts_ref[0].astype(F32)
    degree = 1.0 + jnp.sum(jnp.sum(counts, axis=0), axis=1, keepdims=True)
    grad = jnp.where(preact_ref[...] > 0, cot_ref[...], 0.0)
    feat = feat_ref[...].astype(F32).T.astype(BF16)
    self_ref[...] += dot(jnp.concatenate([feat, feat], axis=1), jnp.concatenate(halves(grad), axis=0))
    both = jnp.concatenate(halves(grad / jnp.sqrt(degree)), axis=0)
    for t in range(0, K, 2):
        pair = jnp.concatenate([counts[t].T, counts[t + 1].T], axis=0).astype(BF16)
        part = dot(jnp.concatenate([pair, pair], axis=1), both)
        for i in range(2):
            c = col_ref[b, t + i]
            started = seen[c] > 0
            seen[c] = 1
            for r in range(PIECES):
                place = column(r, c)
                new = part[i * BLK : (i + 1) * BLK, r * BLK : (r + 1) * BLK]
                acc[place] = jnp.where(started, acc[place], 0.0) + new

    @pl.when(b == BLK_DEV - 1)
    def _():
        row = lax.broadcasted_iota(jnp.int32, (TAG, BLK), 0)
        owners, slots = (jnp.concatenate([ref[...]] * 2, axis=1) for ref in (owner_ref, slot_ref))
        tag = jnp.where(row == 0, owners, jnp.where(row == 1, slots, 0)).astype(F32).astype(BF16)

        @pl.loop(0, OWNERS)
        def _(j):
            for r in range(PIECES):
                start = (r * COLUMNS + BLK_DEV) * PITCH + j
                send_ref[j, r * NB : (r + 1) * NB] = acc[pl.ds(start, NB, stride=PITCH)].astype(BF16)
            send_ref[j, PIECES * NB :] = tag

        for c in range(BLK_DEV):
            for r in range(PIECES):
                own_ref[c * BLK : (c + 1) * BLK, r * BLK : (r + 1) * BLK] = acc[column(r, c)]


def partials(tile_col, counts, preact, cotangent, features, owner, slot):
    rows = pl.BlockSpec((BLK, D), lambda b, *_: (b, 0))
    return pl.pallas_call(
        scatter_kernel,
        grid_spec=pltpu.PrefetchScalarGridSpec(
            num_scalar_prefetch=1,
            grid=(BLK_DEV,),
            in_specs=[
                pl.BlockSpec((1, K, BLK, BLK), lambda b, *_: (b, 0, 0, 0)),
                rows,
                rows,
                rows,
                whole(1, NB),
                whole(1, NB),
            ],
            out_specs=[whole(BLK_DEV * BLK, D), whole(D, D), pl.BlockSpec(memory_space=pltpu.VMEM)],
            scratch_shapes=[
                pltpu.VMEM(((PIECES * COLUMNS + 1) * PITCH, BLK), F32),
                pltpu.SMEM((COLUMNS,), jnp.int32),
            ],
        ),
        out_shape=[
            pltpu.VMEM((BLK_DEV * BLK, D), F32),
            pltpu.VMEM((D, D), F32),
            pltpu.VMEM((OWNERS, SENT, BLK), BF16),
        ],
        compiler_params=pltpu.CompilerParams(vmem_limit_bytes=50 << 20),
        cost_estimate=pl.CostEstimate(
            flops=4 * BLK_DEV * K * BLK * BLK * D, bytes_accessed=22 << 20, transcendentals=0
        ),
    )(tile_col, counts, preact, cotangent, features, owner, slot)


GROUP = 64
STEPS = OWNERS // GROUP
BINS = OWNERS * BLK_DEV
MERGED = 256


def merge_kernel(recv_ref, out_ref, acc):
    step = pl.program_id(0)

    @pl.when(step == 0)
    def _():
        acc[...] = jnp.zeros_like(acc)

    pieces = [recv_ref[:, r * NB : (r + 1) * NB].reshape(GROUP * NB, BLK) for r in range(PIECES)]
    values = jnp.concatenate(pieces, axis=1)
    lists = [recv_ref[i, PIECES * NB :].astype(F32) for i in range(GROUP)]
    numbers = [rows[:1] * BLK_DEV + rows[1:2] for rows in lists]
    first = lax.broadcasted_iota(jnp.int32, (1, BLK), 1) < NB
    pairs = [jnp.where(first, numbers[i], numbers[i + 1]).astype(jnp.int32) for i in range(0, GROUP, 2)]
    rows = lax.broadcasted_iota(jnp.int32, (MERGED, BLK), 0)
    for m in range(0, BINS, MERGED):
        hot = [jnp.where(rows == pair - m, 1.0, 0.0).astype(BF16) for pair in pairs]
        acc[m : m + MERGED] += dot(jnp.concatenate(hot, axis=1), values)

    @pl.when(step == STEPS - 1)
    def _():
        out_ref[...] = acc[...].astype(BF16)


def merged(received):
    return pl.pallas_call(
        merge_kernel,
        grid=(STEPS,),
        in_specs=[pl.BlockSpec((GROUP, SENT, BLK), lambda s: (s, 0, 0))],
        out_specs=whole(BINS, PIECES * BLK),
        out_shape=jax.ShapeDtypeStruct((BINS, PIECES * BLK), BF16),
        scratch_shapes=[pltpu.VMEM((BINS, PIECES * BLK), F32)],
        compiler_params=pltpu.CompilerParams(vmem_limit_bytes=32 << 20),
        cost_estimate=pl.CostEstimate(
            flops=2 * BINS * OWNERS * NB * PIECES * BLK, bytes_accessed=10 << 20, transcendentals=0
        ),
    )(received)


def add_own(recv_ref, own_ref, flat, total):
    arrived = recv_ref[...].astype(F32).reshape(BINS, D)
    for r in range(PIECES):
        flat[r * BINS : (r + 1) * BINS] = arrived[:, r * BLK : (r + 1) * BLK]
    for g in range(BLK_DEV):
        for r in range(PIECES):
            place = slice(g * BLK, (g + 1) * BLK), slice(r * BLK, (r + 1) * BLK)
            total[place] = own_ref[place] + flat[pl.ds(r * BINS + g, OWNERS, stride=BLK_DEV)]


def neigh_kernel(recv_ref, own_ref, feat_ref, self_ref, joined_ref, flat, total):
    add_own(recv_ref, own_ref, flat, total)
    neigh = jnp.zeros((D, D), F32)
    for g in range(0, BLK_DEV * BLK, 2 * BLK):
        upper, lower = halves(total[g : g + 2 * BLK])
        feat = feat_ref[g : g + 2 * BLK].astype(F32).T.astype(BF16)
        neigh += dot(feat, upper) + dot(feat, lower)
    joined_ref[:D] = self_ref[...].astype(BF16)
    joined_ref[D:] = neigh.astype(BF16)


VMEM_SPEC = pl.BlockSpec(memory_space=pltpu.VMEM)
TOTAL_SCRATCH = [pltpu.VMEM((PIECES * BINS + BLK_DEV, BLK), F32), pltpu.VMEM((BLK_DEV * BLK, D), F32)]


def weight_gradients(received, own, features, self_part):
    return pl.pallas_call(
        neigh_kernel,
        in_specs=[VMEM_SPEC] * 4,
        out_specs=VMEM_SPEC,
        out_shape=jax.ShapeDtypeStruct((2 * D, D), BF16),
        scratch_shapes=TOTAL_SCRATCH,
        compiler_params=pltpu.CompilerParams(vmem_limit_bytes=32 << 20),
        cost_estimate=pl.CostEstimate(
            flops=4 * BLK_DEV * BLK * D * D, bytes_accessed=6 << 20, transcendentals=0
        ),
    )(received, own, features, self_part)


def share_kernel(shares_ref, spread_ref):
    share = jnp.sum(shares_ref[...].astype(F32), axis=0, keepdims=True).astype(BF16)
    spread_ref[...] = jnp.broadcast_to(share, spread_ref.shape)


def added_up(shares):
    return pl.pallas_call(
        share_kernel,
        in_specs=[VMEM_SPEC],
        out_specs=VMEM_SPEC,
        out_shape=jax.ShapeDtypeStruct(shares.shape, BF16),
        compiler_params=pltpu.CompilerParams(vmem_limit_bytes=16 << 20),
    )(shares)


def feature_kernel(recv_ref, own_ref, preact_ref, cot_ref, self_ref, neigh_ref, grad_ref, flat, total):
    g = pl.program_id(0)

    @pl.when(g == 0)
    def _():
        add_own(recv_ref, own_ref, flat, total)

    grad = jnp.where(preact_ref[...] > 0, cot_ref[...], 0.0)
    upper, lower = halves(grad)
    w_upper, w_lower = halves(self_ref[...].T)
    result = dot(upper, w_upper) + dot(lower, w_upper) + dot(upper, w_lower)
    upper, lower = halves(total[pl.ds(pl.multiple_of(2 * BLK * g, BLK), 2 * BLK)])
    w_upper, w_lower = halves(neigh_ref[...].T)
    grad_ref[...] = result + (dot(upper, w_upper) + dot(lower, w_upper) + dot(upper, w_lower))


def feature_gradient(received, own, preact, cotangent, w_self, w_neigh):
    rows = pl.BlockSpec((2 * BLK, D), lambda g: (g, 0))
    return pl.pallas_call(
        feature_kernel,
        grid=(BLK_DEV // 2,),
        in_specs=[
            whole(OWNERS, BLK_DEV, PIECES * BLK),
            whole(BLK_DEV * BLK, D),
            rows,
            rows,
            whole(D, D),
            whole(D, D),
        ],
        out_specs=rows,
        out_shape=jax.ShapeDtypeStruct((BLK_DEV * BLK, D), F32),
        scratch_shapes=TOTAL_SCRATCH,
        compiler_params=pltpu.CompilerParams(vmem_limit_bytes=20 << 20),
        cost_estimate=pl.CostEstimate(
            flops=12 * BLK_DEV * BLK * D * D, bytes_accessed=10 << 20, transcendentals=0
        ),
    )(received, own, preact, cotangent, w_self, w_neigh)


def shards(features, preact, cotangent, w_self, w_neigh, tile_counts, tile_col, owner, slot):
    own, self_part, outgoing = partials(tile_col, tile_counts, preact, cotangent, features, owner, slot)
    received = lax.all_to_all(outgoing, "nodes", 0, 0, tiled=True)
    sums = merged(received).reshape(OWNERS, BLK_DEV, PIECES * BLK)
    sums = lax.all_to_all(sums, "nodes", 0, 0, tiled=True)
    joined = weight_gradients(sums, own, features, self_part)

    joined, sums = lax.optimization_barrier((joined, sums))
    rows = 2 * D // OWNERS
    shares = lax.all_to_all(joined.reshape(OWNERS, rows, D), "nodes", 0, 0, tiled=True)
    grad_features = feature_gradient(sums, own, preact, cotangent, w_self, w_neigh)
    spread, grad_features = lax.optimization_barrier((added_up(shares), grad_features))
    both = lax.all_to_all(spread, "nodes", 0, 0, tiled=True).reshape(2 * D, D)
    scale = 1.0 / math.sqrt(OWNERS * BLK_DEV * BLK)
    return grad_features, both[:D].astype(F32) * scale, both[D:].astype(F32) * scale


def solution(mesh):
    rows = P("nodes", None)
    return jax.shard_map(
        shards,
        mesh=mesh,
        in_specs=(rows, rows, rows, P(), P(), P("nodes", None, None, None), rows, rows, rows),
        out_specs=(rows, P(), P()),
        check_vma=False,
    )
```
